32 devices in a mesh: dp: 4 (over y, core), row: 2 (over x), col: 4 (over z).
Axes of the slice: x: 2, y: 2, z: 4, core: 2. Of those that a mesh axis runs over, the one named last changes fastest.
Arguments:
- tokens: bfloat16 [256, 6144], P(('dp', 'row', 'col')), may hold values from -6 to 6
- w_in: bfloat16 [6144, 4, 3072], P('row', 'col'), may hold values from -0.078125 to 0.078125
- w_out: bfloat16 [4, 3072, 6144], P('col', None, 'row'), may hold values from -0.0546875 to 0.0546875
- grad_out: bfloat16 [256, 6144], P(('dp', 'col'), 'row'), may hold values from -6 to 6
Outputs:
- block_out: bfloat16 [256, 6144], P(('dp', 'col'), 'row')
- grad_in: bfloat16 [256, 6144], P(('dp', 'col'), 'row')
- grad_w_in: bfloat16 [6144, 4, 3072], P('row', 'col', 'dp')
- grad_w_out: bfloat16 [4, 3072, 6144], P('col', 'dp', 'row')
The draws below stay inside these ranges and needn't reach their ends.
All inputs are finite; a program needn't handle non-finite values.
Results may differ from the reference program's by a relative error of at most 0.015.
Values may be sent and summed in bfloat16 or wider, within the bound.
No kernel may reach another device: no remote copies, remote signals or barrier semaphores. Data moves between devices by JAX's collectives and lax.ppermute only.
A program may use at most 192 MiB of HBM per device.

```python
import jax
import jax.numpy as jnp
from jax import lax

D = 6144
FF = 12288
TOKENS = 256
HID_COL = 3072
N_COL = 4


def block_scale(key, shape, shards, least, high):
    level = 1.0
    for position, parts in shards:
        steps = jax.random.uniform(jax.random.fold_in(jax.random.fold_in(key, 6), position), (parts,), jnp.float32, least / len(shards), high / len(shards))
        level = level * jnp.repeat(jnp.exp(steps), shape[position] // parts).reshape((-1,) + (1,) * (len(shape) - 1 - position))
    return level


def scatter_about(key, dims, spread, reach, shards=(), dtype=jnp.bfloat16):
    drawn = jax.random.normal(key, dims, jnp.float32) * spread
    if len(shards) > 0:
        drawn = block_scale(key, dims, shards, -0.22, 0.18) * drawn
    return jnp.clip(drawn, min=-reach, max=reach).astype(dtype)


def setup_inputs(seed: int = 0) -> dict:
    arg_keys = jax.random.split(jax.random.key(seed), 5)
    tokens = scatter_about(arg_keys[0], (TOKENS, D), 1.0, 6.0, ((0, 32),))
    w_in = scatter_about(arg_keys[1], (D, N_COL, HID_COL), D ** -0.5, 0.078125, ((0, 2), (1, 4)))
    w_out = scatter_about(arg_keys[2], (N_COL, HID_COL, D), FF ** -0.5, 0.0546875, ((0, 4), (2, 2)))
    grad_out = scatter_about(arg_keys[3], (TOKENS, D), 1.0, 6.0, ((0, 16), (1, 2)))
    return dict(tokens=tokens, w_in=w_in, w_out=w_out, grad_out=grad_out)


def gelu_parts(preact):
    cdf = 0.5 * (1.0 + lax.erf(preact * 0.7071067811865476))
    slopes = cdf + preact * jnp.exp(-0.5 * preact * preact) * 0.3989422804014327
    return preact * cdf, slopes


def reference(tokens, w_in, w_out, grad_out):
    w_first = w_in.reshape(D, FF)
    w_second = w_out.reshape(FF, D)
    preact = jnp.dot(tokens, w_first, preferred_element_type=jnp.float32)
    gelu_out, slopes = gelu_parts(preact)
    hidden = gelu_out.astype(jnp.bfloat16)
    block_out = jnp.dot(hidden, w_second, preferred_element_type=jnp.float32).astype(jnp.bfloat16)
    back_hid = lax.dot_general(grad_out, w_second, (((1,), (1,)), ((), ())), preferred_element_type=jnp.float32)
    grad_pre = (back_hid * slopes).astype(jnp.bfloat16)
    grad_in = lax.dot_general(grad_pre, w_first, (((1,), (1,)), ((), ())), preferred_element_type=jnp.float32).astype(jnp.bfloat16)
    sum_in = lax.dot_general(tokens, grad_pre, (((0,), (0,)), ((), ())), preferred_element_type=jnp.float32)
    sum_out = lax.dot_general(hidden, grad_out, (((0,), (0,)), ((), ())), preferred_element_type=jnp.float32)
    grad_w_in = sum_in.astype(jnp.bfloat16).reshape(D, N_COL, FF // N_COL)
    grad_w_out = sum_out.astype(jnp.bfloat16).reshape(N_COL, FF // N_COL, D)
    return block_out, grad_in, grad_w_in, grad_w_out
```

```python
import functools

import jax
import jax.numpy as jnp
from jax import lax
from jax.experimental import pallas as pl
from jax.experimental.pallas import tpu as pltpu
from jax.sharding import PartitionSpec as P

CORES = 2
VMEM_LIMIT = 60 * 1024 * 1024
NT = (((1,), (1,)), ((), ()))
NN = (((1,), (0,)), ((), ()))
TN = (((0,), (0,)), ((), ()))


def mm(a, b, dims):
    return lax.dot_general(a, b, dims, preferred_element_type=jnp.float32)


def tile_of(size, most):
    for tile in range(most, 0, -128):
        if size % tile == 0:
            return tile
    return size


def whole(*shape):
    return pl.BlockSpec(shape, lambda *_: (0,) * len(shape))


def call(kernel, grid, in_specs, out_specs, out_shape, scratch, name, flops, size, idx, *args):
    return pl.pallas_call(
        kernel,
        grid_spec=pltpu.PrefetchScalarGridSpec(
            num_scalar_prefetch=1,
            grid=grid,
            in_specs=in_specs,
            out_specs=out_specs,
            scratch_shapes=scratch,
        ),
        out_shape=out_shape,
        compiler_params=pltpu.CompilerParams(vmem_limit_bytes=VMEM_LIMIT),
        cost_estimate=pl.CostEstimate(flops=flops, bytes_accessed=size, transcendentals=0),
        name=name,
    )(idx, *args)


def first_kernel(dims, idx, own, other, w, total, sent, rows):
    half = own.shape[0]

    @pl.when((pl.program_id(0) == 0) & (pl.program_id(1) == 0))
    def _():
        rows[:half] = own[...]
        rows[half:] = other[...]

    part = mm(rows[...], w[...], dims)
    total[...] = part
    sent[...] = part.astype(jnp.bfloat16)


def first(idx, own, other, w, blocks, size, transposed, name):
    half, width = own.shape
    tile = tile_of(size, 256)
    per = size // tile
    n = 2 * half
    if transposed:
        w_spec = pl.BlockSpec((tile, width), lambda b, j, idx: (idx[b] * per + j, 0))
    else:
        w_spec = pl.BlockSpec((width, tile), lambda b, j, idx: (0, idx[b] * per + j))
    out_spec = pl.BlockSpec((n, tile), lambda b, j, idx: (0, b * per + j))
    return call(
        functools.partial(first_kernel, NT if transposed else NN),
        (blocks, per),
        [whole(half, width), whole(half, width), w_spec],
        [out_spec, out_spec],
        [
            jax.ShapeDtypeStruct((n, blocks * size), jnp.float32),
            jax.ShapeDtypeStruct((n, blocks * size), jnp.bfloat16),
        ],
        [pltpu.VMEM((n, width), jnp.bfloat16)],
        name,
        2 * n * width * blocks * size,
        2 * width * blocks * size,
        idx,
        own,
        other,
        w,
    )


def gelu_parts(preact):
    cdf = 0.5 * (1.0 + lax.erf(preact * 0.7071067811865476))
    slopes = cdf + preact * jnp.exp(-0.5 * preact * preact) * 0.3989422804014327
    return (preact * cdf, slopes)


def second_product(blocks, size, dims, vals, weights, keep, send):
    half = keep.shape[0]
    part = mm(vals[:, :size], weights[0][...], dims)
    for b in range(1, blocks):
        part += mm(vals[:, b * size : (b + 1) * size], weights[b][...], dims)
    keep[...] = part[:half]
    send[...] = part[half:].astype(jnp.bfloat16)


def forward_kernel(blocks, size, shares, idx, *refs):
    total, parts = refs[0], refs[1 : 1 + shares]
    weights = refs[1 + shares : 1 + shares + blocks]
    keep, send, slopes, *hidden, vals = refs[1 + shares + blocks :]

    @pl.when(pl.program_id(0) == 0)
    def _():
        for b in range(blocks):
            cut = slice(b * size, (b + 1) * size)
            preact = total[:, cut]
            for part in parts:
                preact = preact + part[:, cut].astype(jnp.float32)
            value, slope = gelu_parts(preact)
            value = value.astype(jnp.bfloat16)
            vals[:, cut] = value
            hidden[b][...] = value
            slopes[:, cut] = slope

    second_product(blocks, size, NN, vals, weights, keep, send)


def backward_kernel(blocks, size, shares, idx, *refs):
    total, parts = refs[0], refs[1 : 1 + shares]
    slopes = refs[1 + shares]
    weights = refs[2 + shares : 2 + shares + blocks]
    keep, send, *pre, vals = refs[2 + shares + blocks :]

    @pl.when(pl.program_id(0) == 0)
    def _():
        for b in range(blocks):
            cut = slice(b * size, (b + 1) * size)
            back = total[:, cut]
            for part in parts:
                back = back + part[:, cut].astype(jnp.float32)
            value = (back * slopes[:, cut]).astype(jnp.bfloat16)
            vals[:, cut] = value
            pre[b][...] = value

    second_product(blocks, size, NT, vals, weights, keep, send)


def second(idx, total, parts, slopes, w, blocks, size, width, name):
    n = total.shape[0]
    half = n // 2
    tile = tile_of(width, 512)
    forward = slopes is None
    if forward:
        w_specs = [
            pl.BlockSpec((size, tile), functools.partial(lambda b, j, idx: (idx[b], j), b))
            for b in range(blocks)
        ]
    else:
        w_specs = [
            pl.BlockSpec((tile, size), functools.partial(lambda b, j, idx: (j, idx[b]), b))
            for b in range(blocks)
        ]
    acts = whole(n, blocks * size)
    out_spec = pl.BlockSpec((half, tile), lambda j, idx: (0, j))
    out_specs = [out_spec, out_spec]
    out_shape = [
        jax.ShapeDtypeStruct((half, width), jnp.float32),
        jax.ShapeDtypeStruct((half, width), jnp.bfloat16),
    ]
    if forward:
        out_specs.append(acts)
        out_shape.append(jax.ShapeDtypeStruct((n, blocks * size), jnp.float32))
    out_specs += [whole(n, size)] * blocks
    out_shape += [jax.ShapeDtypeStruct((n, size), jnp.bfloat16)] * blocks
    extra = [] if forward else [slopes]
    return call(
        functools.partial(
            forward_kernel if forward else backward_kernel, blocks, size, len(parts)
        ),
        (width // tile,),
        [acts] * (1 + len(parts) + len(extra)) + w_specs,
        out_specs,
        out_shape,
        [pltpu.VMEM((n, blocks * size), jnp.bfloat16)],
        name,
        2 * n * width * blocks * size,
        2 * width * blocks * size,
        idx,
        total,
        *parts,
        *extra,
        *[w] * blocks,
    )


def weight_kernel(groups, idx, *refs):
    left, right, out = refs[:groups], refs[groups : 2 * groups], refs[2 * groups]
    total = None
    for a, b in zip(left, right):
        part = mm(a[...], b[...], TN)
        total = part if total is None else total + part
    out[...] = total.astype(jnp.bfloat16)


def weight_grad(idx, left, right, rows_tiled, name):
    n = left[0].shape[0]
    k, m = left[0].shape[1], right[0].shape[1]
    if rows_tiled:
        tile = tile_of(k, 512)
        grid = (k // tile,)
        left_spec = pl.BlockSpec((n, tile), lambda j, idx: (0, j))
        right_spec = whole(n, m)
        out_spec = pl.BlockSpec((tile, m), lambda j, idx: (j, 0))
    else:
        tile = tile_of(m, 512)
        grid = (m // tile,)
        left_spec = whole(n, k)
        right_spec = pl.BlockSpec((n, tile), lambda j, idx: (0, j))
        out_spec = pl.BlockSpec((k, tile), lambda j, idx: (0, j))
    groups = len(left)
    return call(
        functools.partial(weight_kernel, groups),
        grid,
        [left_spec] * groups + [right_spec] * groups,
        out_spec,
        jax.ShapeDtypeStruct((k, m), jnp.bfloat16),
        [],
        name,
        2 * n * groups * k * m,
        2 * k * m,
        idx,
        *left,
        *right,
    )


def body(dp, row, col, tokens, w_in, w_out, grad_out):
    blocks = dp // CORES
    w_first = w_in[:, 0, :]
    w_second = w_out[0]
    width = w_first.shape[0]
    size = w_first.shape[1] // dp
    mine = lax.axis_index("dp")
    idx = jnp.stack([(mine + CORES * b) % dp for b in range(blocks)]).astype(jnp.int32)

    other_core = [(i, i ^ 1) for i in range(dp)]

    def across_cores(x):
        return lax.ppermute(x, "dp", other_core)

    def across_y(x, step):
        return lax.ppermute(x, "dp", [(i, (i + CORES * step) % dp) for i in range(dp)])

    def across_rows(x):
        return [
            lax.ppermute(x, "row", [(i, (i + step) % row) for i in range(row)])
            for step in range(1, row)
        ]

    n = tokens.shape[0]
    spread = tokens.reshape(n, row, width).swapaxes(0, 1)
    spread = jnp.broadcast_to(spread[:, None], (row, col, n, width)).reshape(row * col, n, width)
    tok = lax.all_to_all(spread, ("row", "col"), 0, 0, tiled=True).reshape(row * col * n, width)
    m = grad_out.shape[0]
    spread_out = jnp.broadcast_to(grad_out[None], (col, m, width))
    cot = lax.all_to_all(spread_out, "col", 0, 0, tiled=True).reshape(col * m, width)

    tok_other = across_cores(tok)
    pre_total, pre_sent = first(
        idx, tok, tok_other, w_first, blocks, size, False, "preact_partial"
    )
    pre_parts = across_rows(pre_sent)
    cot_other = across_cores(cot)
    back_total, back_sent = first(
        idx, cot, cot_other, w_second, blocks, size, True, "back_partial"
    )
    back_parts = across_rows(back_sent)

    def col_total(keep, send):
        terms = (keep + across_cores(send).astype(jnp.float32)).astype(jnp.bfloat16)
        terms = lax.all_to_all(terms.reshape(col, m, width), "col", 0, 0, tiled=True)
        return jnp.sum(terms.astype(jnp.float32), axis=0).astype(jnp.bfloat16)

    keep, send, slopes, *hidden = second(
        idx, pre_total, pre_parts, None, w_second, blocks, size, width, "block_out_partial"
    )
    block_out = col_total(keep, send)
    keep, send, *grad_pre = second(
        idx, back_total, back_parts, slopes, w_first, blocks, size, width, "grad_in_partial"
    )
    grad_in = col_total(keep, send)

    def all_replicas(own, other):
        groups = [own, other]
        for b in range(1, blocks):
            there = across_y(own, b)
            groups += [there, across_cores(there)]
        return groups

    def halves(x):
        return [x[: x.shape[0] // 2], x[x.shape[0] // 2 :]]

    def to_owner(parts):
        out = halves(parts[0])
        for b in range(1, blocks):
            out += halves(across_y(parts[b], b))
        return out

    cot_all = all_replicas(cot, cot_other)
    tok_all = all_replicas(tok, tok_other)
    hid_mine = to_owner(hidden)
    pre_mine = to_owner(grad_pre)
    grad_out_w = weight_grad(idx, hid_mine, cot_all, False, "grad_w_out")
    grad_in_w = weight_grad(idx, tok_all, pre_mine, True, "grad_w_in")
    return block_out, grad_in, grad_in_w[:, None, :], grad_out_w[None]


def solution(mesh):
    in_specs = (
        P(("dp", "row", "col"), None),
        P("row", "col", None),
        P("col", None, "row"),
        P(("dp", "col"), "row"),
    )
    out_specs = (
        P(("dp", "col"), "row"),
        P(("dp", "col"), "row"),
        P("row", "col", "dp"),
        P("col", "dp", "row"),
    )
    sizes = (mesh.shape["dp"], mesh.shape["row"], mesh.shape["col"])
    return jax.shard_map(
        functools.partial(body, *sizes),
        mesh=mesh,
        in_specs=in_specs,
        out_specs=out_specs,
        check_vma=False,
    )
```

```python
import functools

import jax
import jax.numpy as jnp
from jax import lax
from jax.experimental import pallas as pl
from jax.experimental.pallas import tpu as pltpu
from jax.sharding import PartitionSpec as P

CORES = 2
MIB = 1024 * 1024
NT = (((1,), (1,)), ((), ()))
NN = (((1,), (0,)), ((), ()))
TN = (((0,), (0,)), ((), ()))
VMEM = pl.BlockSpec(memory_space=pltpu.VMEM)
SMEM = pl.BlockSpec(memory_space=pltpu.SMEM)
HBM = pl.BlockSpec(memory_space=pltpu.HBM)


def mm(a, b, dims):
    return lax.dot_general(a, b, dims, preferred_element_type=jnp.float32)


def tile_of(size, most):
    for tile in range(most, 0, -128):
        if size % tile == 0:
            return tile
    return size


def call(kernel, in_specs, out_specs, out_shape, name, flops=0, size=0, scratch=(), limit=24):
    return pl.pallas_call(
        kernel,
        in_specs=in_specs,
        out_specs=out_specs,
        out_shape=out_shape,
        scratch_shapes=scratch,
        compiler_params=pltpu.CompilerParams(vmem_limit_bytes=limit * MIB),
        cost_estimate=pl.CostEstimate(flops=flops, bytes_accessed=size, transcendentals=0),
        name=name,
    )


def shape(dims, dtype=jnp.bfloat16):
    return jax.ShapeDtypeStruct(tuple(dims), dtype)


def load_kernel(blocks, size, pieces, place, w_first, w_second, first, second, sems):
    width = w_first.shape[0]
    copies = []
    for b in range(blocks):
        at = pl.multiple_of(place[b] * size, 128)
        for p in range(pieces):
            rows = pl.ds(p * (width // pieces), width // pieces)
            copies.append((w_first.at[rows, pl.ds(at, size)], first.at[b, rows]))
    for b in range(blocks):
        for p in range(pieces):
            rows = pl.ds(p * (size // pieces), size // pieces)
            at = pl.multiple_of(place[b] * size + p * (size // pieces), 16)
            copies.append((w_second.at[pl.ds(at, size // pieces)], second.at[b, rows]))
    copies = [pltpu.make_async_copy(a, b, sems.at[i]) for i, (a, b) in enumerate(copies)]
    for copy in copies:
        copy.start()
    for copy in copies:
        copy.wait()


def load(place, w_first, w_second, blocks, size):
    width = w_first.shape[0]
    pieces = 4
    return call(
        functools.partial(load_kernel, blocks, size, pieces),
        [SMEM, HBM, HBM],
        [VMEM, VMEM],
        [
            pltpu.VMEM((blocks, width, size), jnp.bfloat16),
            pltpu.VMEM((blocks, size, width), jnp.bfloat16),
        ],
        "load_weights",
        size=8 * blocks * width * size,
        scratch=[pltpu.SemaphoreType.DMA((2 * blocks * pieces,))],
        limit=20,
    )(place, w_first, w_second)


def order_kernel(place, *refs):
    parts, out = refs[:-1], refs[-1]
    count = len(parts)
    rows = parts[0].shape[0]
    me = place[0]
    for k, part in enumerate(parts):
        at = lax.rem(me + count - k, count) * rows
        out[pl.ds(pl.multiple_of(at, 16), rows)] = part[...]


def in_order(col_place, parts):
    rows, width = parts[0].shape
    return call(
        order_kernel,
        [SMEM] + [VMEM] * len(parts),
        VMEM,
        shape((rows * len(parts), width)),
        "order_rows",
        size=4 * rows * len(parts) * width,
    )(col_place, *parts)


def first_kernel(dims, own, other, w, total, sent, rows):
    half = own.shape[0]
    rows[:half] = own[...]
    rows[half:] = other[...]
    blocks = w.shape[0]
    size = total.shape[1] // blocks
    tile = tile_of(size, 256)
    for b in range(blocks):
        for at in range(0, size, tile):
            weight = w[b, :, at : at + tile] if dims is NN else w[b, at : at + tile, :]
            part = mm(rows[...], weight, dims)
            cut = slice(b * size + at, b * size + at + tile)
            total[:, cut] = part
            sent[:, cut] = part.astype(jnp.bfloat16)


def first(own, other, w, size, dims, name):
    half, width = own.shape
    n = 2 * half
    units = w.shape[0] * size
    return call(
        functools.partial(first_kernel, dims),
        [VMEM] * 3,
        [VMEM] * 2,
        [shape((n, units), jnp.float32), shape((n, units))],
        name,
        flops=2 * n * width * units,
        size=2 * width * units,
        scratch=[pltpu.VMEM((n, width), jnp.bfloat16)],
    )(own, other, w)


def gelu_parts(preact):
    cdf = 0.5 * (1.0 + lax.erf(preact * 0.7071067811865476))
    slopes = cdf + preact * jnp.exp(-0.5 * preact * preact) * 0.3989422804014327
    return (preact * cdf, slopes)


def second_product(dims, vals, w, keep, send):
    half, width = keep.shape
    blocks = w.shape[0]
    size = vals.shape[1] // blocks
    tile = tile_of(width, 512)
    for at in range(0, width, tile):
        cut = slice(at, at + tile)
        part = None
        for b in range(blocks):
            weight = w[b, :, cut] if dims is NN else w[b, cut, :]
            term = mm(vals[:, b * size : (b + 1) * size], weight, dims)
            part = term if part is None else part + term
        keep[:, cut] = part[:half]
        send[:, cut] = part[half:].astype(jnp.bfloat16)


def row_sum(total, parts, cut):
    whole = total[:, cut]
    for part in parts:
        whole = whole + part[:, cut].astype(jnp.float32)
    return whole


def forward_kernel(blocks, shares, *refs):
    total, parts, w = refs[0], refs[1 : 1 + shares], refs[1 + shares]
    keep, send, slopes, *hidden, vals = refs[2 + shares :]
    size = total.shape[1] // blocks
    for b in range(blocks):
        cut = slice(b * size, (b + 1) * size)
        value, slope = gelu_parts(row_sum(total, parts, cut))
        value = value.astype(jnp.bfloat16)
        vals[:, cut] = value
        hidden[b][...] = value
        slopes[:, cut] = slope
    second_product(NN, vals, w, keep, send)


def backward_kernel(blocks, shares, *refs):
    total, parts, slopes, w = refs[0], refs[1 : 1 + shares], refs[1 + shares], refs[2 + shares]
    keep, send, *pre, vals = refs[3 + shares :]
    size = total.shape[1] // blocks
    for b in range(blocks):
        cut = slice(b * size, (b + 1) * size)
        value = (row_sum(total, parts, cut) * slopes[:, cut]).astype(jnp.bfloat16)
        vals[:, cut] = value
        pre[b][...] = value
    second_product(NT, vals, w, keep, send)


def second(total, parts, slopes, w, size, name):
    n, units = total.shape
    half = n // 2
    blocks = w.shape[0]
    forward = slopes is None
    width = w.shape[2] if forward else w.shape[1]
    out_shape = [shape((half, width), jnp.float32), shape((half, width))]
    if forward:
        out_shape.append(shape((n, units), jnp.float32))
    out_shape += [shape((n, size))] * blocks
    extra = [] if forward else [slopes]
    return call(
        functools.partial(forward_kernel if forward else backward_kernel, blocks, len(parts)),
        [VMEM] * (2 + len(parts) + len(extra)),
        [VMEM] * len(out_shape),
        out_shape,
        name,
        flops=2 * n * width * units,
        size=2 * width * units,
        scratch=[pltpu.VMEM((n, units), jnp.bfloat16)],
    )(total, *parts, *extra, w)


def cores_kernel(place, keep, part, own, *sent):
    count = 1 + len(sent)
    rows = own.shape[0]
    me = place[0]
    for k in range(count):
        at = pl.ds(pl.multiple_of(lax.rem(me + k, count) * rows, 16), rows)
        whole = keep[at] + part[at].astype(jnp.float32)
        if k == 0:
            own[...] = whole
        else:
            sent[k - 1][...] = whole.astype(jnp.bfloat16)


def cores_sum(col_place, keep, part, count, name):
    rows, width = keep.shape[0] // count, keep.shape[1]
    return call(
        cores_kernel,
        [SMEM, VMEM, VMEM],
        [VMEM] * count,
        [shape((rows, width), jnp.float32)] + [shape((rows, width))] * (count - 1),
        name,
        size=8 * count * rows * width,
    )(col_place, keep, part)


def weight_kernel(lefts, tile, across, *refs):
    left, right, out = refs[:lefts], refs[lefts:-5], refs[-5]
    rows_left, rows_right, staged, sems = refs[-4:]
    for groups, rows in ((left, rows_left), (right, rows_right)):
        at = 0
        for group in groups:
            rows[at : at + group.shape[0]] = group[...]
            at += group.shape[0]
    copies = []
    for i, at in enumerate(range(0, out.shape[1 if across else 0], tile)):
        cut = slice(at, at + tile)
        if across:
            part, where = mm(rows_left[...], rows_right[:, cut], TN), (slice(None), cut)
        else:
            part, where = mm(rows_left[:, cut], rows_right[...], TN), (cut, slice(None))
        staged[where] = part.astype(jnp.bfloat16)
        copies.append(pltpu.make_async_copy(staged.at[where], out.at[where], sems.at[i]))
        copies[-1].start()
    for copy in copies:
        copy.wait()


def weight_grad(left, right, across, name):
    n = sum(group.shape[0] for group in left)
    k, m = left[0].shape[1], right[0].shape[1]
    long = m if across else k
    tile = tile_of(long, 512)
    return call(
        functools.partial(weight_kernel, len(left), tile, across),
        [VMEM] * (len(left) + len(right)),
        HBM,
        shape((k, m)),
        name,
        flops=2 * n * k * m,
        size=2 * k * m,
        scratch=[
            pltpu.VMEM((n, k), jnp.bfloat16),
            pltpu.VMEM((n, m), jnp.bfloat16),
            pltpu.VMEM((k, m), jnp.bfloat16),
            pltpu.SemaphoreType.DMA((long // tile,)),
        ],
    )(*left, *right)


def body(dp, row, col, tokens, w_in, w_out, grad_out):
    blocks = dp // CORES
    width, size = w_in.shape[0], w_in.shape[2] // dp
    mine = lax.axis_index("dp")
    place = jnp.stack([(mine + CORES * b) % dp for b in range(blocks)]).astype(jnp.int32)
    col_place = lax.axis_index("col").astype(jnp.int32)[None]

    def shifted(x, axis, step):
        count = {"dp": dp, "row": row, "col": col}[axis]
        return lax.ppermute(x, axis, [(i, (i + step) % count) for i in range(count)])

    def across_cores(x):
        return lax.ppermute(x, "dp", [(i, i ^ 1) for i in range(dp)])

    def across_rows(x):
        return [shifted(x, "row", step) for step in range(1, row)]

    n = tokens.shape[0]
    spread = tokens.reshape(n, row, width).swapaxes(0, 1)
    spread = jnp.broadcast_to(spread[:, None], (row, col, n, width)).reshape(row * col, n, width)
    tok = lax.all_to_all(spread, ("row", "col"), 0, 0, tiled=True).reshape(row * col * n, width)
    cots = [grad_out] + [shifted(grad_out, "col", step) for step in range(1, col)]
    w_first, w_second = load(place, w_in[:, 0, :], w_out[0], blocks, size)
    cot = in_order(col_place, cots)

    tok_other = across_cores(tok)
    pre_total, pre_sent = first(tok, tok_other, w_first, size, NN, "preact_partial")
    pre_parts = across_rows(pre_sent)
    cot_other = across_cores(cot)
    back_total, back_sent = first(cot, cot_other, w_second, size, NT, "back_partial")
    back_parts = across_rows(back_sent)

    def col_total(keep, send, name):
        own, *sent = cores_sum(col_place, keep, across_cores(send), col, name)
        for step, part in enumerate(sent):
            own = own + shifted(part, "col", step + 1).astype(jnp.float32)
        return own.astype(jnp.bfloat16)

    keep, send, slopes, *hidden = second(
        pre_total, pre_parts, None, w_second, size, "block_out_partial"
    )
    block_out = col_total(keep, send, "block_out_cores")
    keep, send, *grad_pre = second(
        back_total, back_parts, slopes, w_first, size, "grad_in_partial"
    )
    grad_in = col_total(keep, send, "grad_in_cores")

    def all_replicas(own, other):
        groups = [own, other]
        for b in range(1, blocks):
            there = shifted(own, "dp", CORES * b)
            groups += [there, across_cores(there)]
        return groups

    def to_owner(parts):
        return [parts[0]] + [shifted(parts[b], "dp", CORES * b) for b in range(1, blocks)]

    cot_all = all_replicas(cot, cot_other)
    tok_all = all_replicas(tok, tok_other)
    grad_out_w = weight_grad(to_owner(hidden), cot_all, True, "grad_w_out")
    grad_in_w = weight_grad(tok_all, to_owner(grad_pre), False, "grad_w_in")
    return block_out, grad_in, grad_in_w[:, None, :], grad_out_w[None]


def solution(mesh):
    in_specs = (
        P(("dp", "row", "col"), None),
        P("row", "col", None),
        P("col", None, "row"),
        P(("dp", "col"), "row"),
    )
    out_specs = (
        P(("dp", "col"), "row"),
        P(("dp", "col"), "row"),
        P("row", "col", "dp"),
        P("col", "dp", "row"),
    )
    sizes = (mesh.shape["dp"], mesh.shape["row"], mesh.shape["col"])
    return jax.shard_map(
        functools.partial(body, *sizes),
        mesh=mesh,
        in_specs=in_specs,
        out_specs=out_specs,
        check_vma=False,
    )
```

```python
import functools

import jax
import jax.numpy as jnp
from jax import lax
from jax.experimental import pallas as pl
from jax.experimental.pallas import tpu as pltpu
from jax.sharding import PartitionSpec as P

CORES = 2
PIECES = 2
MIB = 1024 * 1024
NT = (((1,), (1,)), ((), ()))
NN = (((1,), (0,)), ((), ()))
TN = (((0,), (0,)), ((), ()))
VMEM = pl.BlockSpec(memory_space=pltpu.VMEM)
SMEM = pl.BlockSpec(memory_space=pltpu.SMEM)
HBM = pl.BlockSpec(memory_space=pltpu.HBM)
ANY = pl.BlockSpec(memory_space=pl.ANY)


def mm(a, b, dims):
    return lax.dot_general(a, b, dims, preferred_element_type=jnp.float32)


def tile_of(size, most):
    for tile in range(most, 0, -128):
        if size % tile == 0:
            return tile
    return size


def call(
    kernel, in_specs, out_specs, out_shape, name, scratch=(), limit=24, after=(), cost=0
):
    reads = len(in_specs)

    def run(*refs):
        kernel(*refs[:reads], *refs[reads + len(after) :])

    kernel_call = pl.pallas_call(
        run,
        in_specs=list(in_specs) + [ANY] * len(after),
        out_specs=out_specs,
        out_shape=out_shape,
        scratch_shapes=scratch,
        compiler_params=pltpu.CompilerParams(vmem_limit_bytes=limit * MIB),
        cost_estimate=pl.CostEstimate(flops=0, bytes_accessed=cost * MIB, transcendentals=0),
        name=name,
    )
    return lambda *args: kernel_call(*args, *after)


def shape(dims, dtype=jnp.bfloat16):
    return jax.ShapeDtypeStruct(tuple(dims), dtype)


def load_kernel(blocks, size, pieces, place, w_first, w_second, first, second, sems):
    width = w_first.shape[0]
    copies = []
    for b in range(blocks):
        at = pl.multiple_of(place[b] * size, 128)
        for p in range(pieces):
            rows = pl.ds(p * (width // pieces), width // pieces)
            copies.append((w_first.at[rows, pl.ds(at, size)], first.at[b, rows]))
    for b in range(blocks):
        for p in range(pieces):
            rows = pl.ds(p * (size // pieces), size // pieces)
            at = pl.multiple_of(place[b] * size + p * (size // pieces), 16)
            copies.append((w_second.at[pl.ds(at, size // pieces)], second.at[b, rows]))
    copies = [pltpu.make_async_copy(a, b, sems.at[i]) for i, (a, b) in enumerate(copies)]
    for copy in copies:
        copy.start()
    for copy in copies:
        copy.wait()


def load(place, w_first, w_second, blocks, size, after):
    width = w_first.shape[0]
    pieces = 4
    return call(
        functools.partial(load_kernel, blocks, size, pieces),
        [SMEM, HBM, HBM],
        [VMEM, VMEM],
        [
            pltpu.VMEM((blocks, width, size), jnp.bfloat16),
            pltpu.VMEM((blocks, size, width), jnp.bfloat16),
        ],
        "load_weights",
        scratch=[pltpu.SemaphoreType.DMA((2 * blocks * pieces,))],
        limit=20,
        after=after,
    )(place, w_first, w_second)


def split_kernel(place, tokens, cots, cot, *rest):
    *outs, sems = rest
    count, width = len(outs), outs[0].shape[1]
    copies = [pltpu.make_async_copy(cots, cot, sems.at[count])]
    for k in reversed(range(count)):
        at = lax.rem(place[0] + k, count) * width
        source = tokens.at[:, pl.ds(pl.multiple_of(at, 128), width)]
        copies.append(pltpu.make_async_copy(source, outs[k], sems.at[k]))
    for copy in reversed(copies):
        copy.start()
    for copy in copies:
        copy.wait()


def split(row_place, tokens, cots, count):
    rows, width = tokens.shape[0], tokens.shape[1] // count
    return call(
        split_kernel,
        [SMEM, HBM, HBM],
        [VMEM] * (1 + count),
        [shape(cots.shape)] + [shape((rows, width))] * count,
        "split_width",
        scratch=[pltpu.SemaphoreType.DMA((1 + count,))],
    )(row_place, tokens, cots)


def stack_kernel(*refs):
    *parts, cot, out, cot_out = refs
    out[...] = jnp.concatenate([r[...].astype(jnp.float32) for r in parts]).astype(out.dtype)
    cot_out[...] = cot[...]


def stack(parts, cot):
    rows, width = parts[0].shape
    return call(
        stack_kernel,
        [VMEM] * (1 + len(parts)),
        [VMEM] * 2,
        [shape((rows * len(parts), width)), shape(cot.shape)],
        "stack_rows",
    )(*parts, cot)


def tokens_kernel(row, places, *refs):
    stacks, outs, held = refs[: -1 - PIECES], refs[-1 - PIECES : -1], refs[-1]
    col, n = len(stacks), held.shape[1]
    rows_out = outs[0].shape[0]
    my_row, my_col = places[0], places[1]
    for k, part in enumerate(stacks):
        rows = part[...].astype(jnp.float32)
        for r in range(row):
            at = lax.rem(my_row + row - r, row) * col + lax.rem(my_col + col - k, col)
            held[at] = rows[r * n : (r + 1) * n]
    for at in range(0, row * col, 2):
        pair = jnp.concatenate([held[at], held[at + 1]])
        piece, start = divmod(at * n, rows_out)
        outs[piece][start : start + 2 * n] = pair.astype(jnp.bfloat16)


def tokens_in_order(places, stacks, row, after):
    rows, width = stacks[0].shape
    col = len(stacks)
    return call(
        functools.partial(tokens_kernel, row),
        [SMEM] + [VMEM] * col,
        [VMEM] * PIECES,
        [shape((rows * col // PIECES, width))] * PIECES,
        "order_tokens",
        scratch=[pltpu.VMEM((row * col, rows // row, width), jnp.float32)],
        after=after,
    )(places, *stacks)


def order_kernel(place, *refs):
    parts, out = refs[:-1], refs[-1]
    count = len(parts)
    rows = parts[0].shape[0]
    me = place[0]
    for k, part in enumerate(parts):
        at = lax.rem(me + count - k, count) * rows
        out[pl.ds(pl.multiple_of(at, 16), rows)] = part[...]


def in_order(col_place, parts, after):
    rows, width = parts[0].shape
    return call(
        order_kernel,
        [SMEM] + [VMEM] * len(parts),
        VMEM,
        shape((rows * len(parts), width)),
        "order_rows",
        after=after,
        cost=0,
    )(col_place, *parts)


def first_kernel(dims, pieces, *refs):
    groups, w = refs[: 2 * pieces], refs[2 * pieces]
    total, sent, own_out, rows = refs[2 * pieces + 1 :]
    step = groups[0].shape[0]
    for i, group in enumerate(groups):
        rows[i * step : (i + 1) * step] = group[...]
        if i < pieces:
            own_out[i * step : (i + 1) * step] = group[...]
    blocks = w.shape[0]
    size = total.shape[1] // blocks
    tile = tile_of(size, 256)
    for b in range(blocks):
        for at in range(0, size, tile):
            weight = w[b, :, at : at + tile] if dims is NN else w[b, at : at + tile, :]
            part = mm(rows[...], weight, dims)
            cut = slice(b * size + at, b * size + at + tile)
            total[:, cut] = part
            sent[:, cut] = part.astype(jnp.bfloat16)


def first(own, other, w, size, dims, name, after):
    half, width = len(own) * own[0].shape[0], own[0].shape[1]
    n = 2 * half
    units = w.shape[0] * size
    return call(
        functools.partial(first_kernel, dims, len(own)),
        [VMEM] * (2 * len(own) + 1),
        [VMEM] * 3,
        [shape((n, units), jnp.float32), shape((n, units)), shape((half, width))],
        name,
        scratch=[pltpu.VMEM((n, width), jnp.bfloat16)],
        after=after,
    )(*own, *other, w)


def gelu_parts(preact):
    cdf = 0.5 * (1.0 + lax.erf(preact * 0.7071067811865476))
    slopes = cdf + preact * jnp.exp(-0.5 * preact * preact) * 0.3989422804014327
    return (preact * cdf, slopes)


def second_product(dims, vals, w, keep, sends):
    half, width = keep.shape
    blocks = w.shape[0]
    size = vals.shape[1] // blocks
    tile = tile_of(width, 512)
    for at in range(0, width, tile):
        cut = slice(at, at + tile)
        part = None
        for b in range(blocks):
            weight = w[b, :, cut] if dims is NN else w[b, cut, :]
            term = mm(vals[:, b * size : (b + 1) * size], weight, dims)
            part = term if part is None else part + term
        keep[:, cut] = part[:half]
        for i, send in enumerate(sends):
            rows = send.shape[0]
            send[:, cut] = part[half + i * rows : half + (i + 1) * rows].astype(jnp.bfloat16)


def row_sum(total, parts, cut):
    whole = total[:, cut]
    for part in parts:
        whole = whole + part[:, cut].astype(jnp.float32)
    return whole


def forward_kernel(blocks, shares, *refs):
    total, parts, w = refs[0], refs[1 : 1 + shares], refs[1 + shares]
    keep, *sends = refs[2 + shares : 3 + shares + PIECES]
    slopes, *hidden, vals = refs[3 + shares + PIECES :]
    size = total.shape[1] // blocks
    for b in range(blocks):
        cut = slice(b * size, (b + 1) * size)
        value, slope = gelu_parts(row_sum(total, parts, cut))
        value = value.astype(jnp.bfloat16)
        vals[:, cut] = value
        hidden[b][...] = value
        slopes[:, cut] = slope
    second_product(NN, vals, w, keep, sends)


def backward_kernel(blocks, shares, *refs):
    total, parts, slopes, w = refs[0], refs[1 : 1 + shares], refs[1 + shares], refs[2 + shares]
    keep, *sends = refs[3 + shares : 4 + shares + PIECES]
    *pre, vals = refs[4 + shares + PIECES :]
    size = total.shape[1] // blocks
    for b in range(blocks):
        cut = slice(b * size, (b + 1) * size)
        value = (row_sum(total, parts, cut) * slopes[:, cut]).astype(jnp.bfloat16)
        vals[:, cut] = value
        pre[b][...] = value
    second_product(NT, vals, w, keep, sends)


def second(total, parts, slopes, w, size, name, after=()):
    n, units = total.shape
    half = n // 2
    blocks = w.shape[0]
    forward = slopes is None
    width = w.shape[2] if forward else w.shape[1]
    out_shape = [shape((half, width), jnp.float32)] + [shape((half // PIECES, width))] * PIECES
    if forward:
        out_shape.append(shape((n, units), jnp.float32))
    out_shape += [shape((n, size))] * blocks
    extra = [] if forward else [slopes]
    return call(
        functools.partial(forward_kernel if forward else backward_kernel, blocks, len(parts)),
        [VMEM] * (2 + len(parts) + len(extra)),
        [VMEM] * len(out_shape),
        out_shape,
        name,
        scratch=[pltpu.VMEM((n, units), jnp.bfloat16)],
        after=after,
        cost=0,
    )(total, *parts, *extra, w)


def cores_kernel(place, keep, *refs):
    parts, own = refs[:PIECES], refs[PIECES]
    *sent, held = refs[PIECES + 1 :]
    rows = own.shape[0]
    at = 0
    for part in parts:
        cut = slice(at, at + part.shape[0])
        held[cut] = keep[cut] + part[...].astype(jnp.float32)
        at += part.shape[0]
    count = 1 + len(sent)
    me = place[0]
    for k in range(count):
        at = pl.ds(pl.multiple_of(lax.rem(me + k, count) * rows, 16), rows)
        if k == 0:
            own[...] = held[at]
        else:
            sent[k - 1][...] = held[at].astype(jnp.bfloat16)


def cores_sum(col_place, keep, parts, count, name, after=()):
    rows, width = keep.shape[0] // count, keep.shape[1]
    return call(
        cores_kernel,
        [SMEM, VMEM] + [VMEM] * PIECES,
        [VMEM] * count,
        [shape((rows, width), jnp.float32)] + [shape((rows, width))] * (count - 1),
        name,
        scratch=[pltpu.VMEM(keep.shape, jnp.float32)],
        after=after,
    )(col_place, keep, *parts)


def mark_kernel(*refs):
    refs[-1][...] = refs[0][:16, :128]


def mark(parts):
    return call(mark_kernel, [VMEM] * len(parts), VMEM, shape((16, 128)), "mark")(*parts)


def weight_kernel(lefts, tile, across, *refs):
    left, right, out = refs[:lefts], refs[lefts:-5], refs[-5]
    rows_left, rows_right, staged, sems = refs[-4:]
    for groups, rows in ((left, rows_left), (right, rows_right)):
        at = 0
        for group in groups:
            rows[at : at + group.shape[0]] = group[...]
            at += group.shape[0]
    copies = []
    for i, at in enumerate(range(0, out.shape[1 if across else 0], tile)):
        cut = slice(at, at + tile)
        if across:
            part, where = mm(rows_left[...], rows_right[:, cut], TN), (slice(None), cut)
        else:
            part, where = mm(rows_left[:, cut], rows_right[...], TN), (cut, slice(None))
        staged[where] = part.astype(jnp.bfloat16)
        copies.append(pltpu.make_async_copy(staged.at[where], out.at[where], sems.at[i]))
        copies[-1].start()
    for copy in copies:
        copy.wait()


def weight_grad(left, right, across, name, after):
    n = sum(group.shape[0] for group in left)
    k, m = left[0].shape[1], right[0].shape[1]
    long = m if across else k
    tile = tile_of(long, 512)
    return call(
        functools.partial(weight_kernel, len(left), tile, across),
        [VMEM] * (len(left) + len(right)),
        HBM,
        shape((k, m)),
        name,
        scratch=[
            pltpu.VMEM((n, k), jnp.bfloat16),
            pltpu.VMEM((n, m), jnp.bfloat16),
            pltpu.VMEM((k, m), jnp.bfloat16),
            pltpu.SemaphoreType.DMA((long // tile,)),
        ],
        after=after,
        cost=0,
    )(*left, *right)


def body(dp, row, col, tokens, w_in, w_out, grad_out):
    blocks = dp // CORES
    width, size = w_in.shape[0], w_in.shape[2] // dp
    mine = lax.axis_index("dp")
    place = jnp.stack([(mine + CORES * b) % dp for b in range(blocks)]).astype(jnp.int32)
    row_place = lax.axis_index("row").astype(jnp.int32)[None]
    col_place = lax.axis_index("col").astype(jnp.int32)[None]

    def shifted(x, axis, step):
        count = {"dp": dp, "row": row, "col": col}[axis]
        return lax.ppermute(x, axis, [(i, (i + step) % count) for i in range(count)])

    def across_cores(x):
        return lax.ppermute(x, "dp", [(i, i ^ 1) for i in range(dp)])

    def across_rows(x):
        return [shifted(x, "row", step) for step in range(1, row)]

    def all_replicas(own, other, there):
        groups = [own, *other]
        for part in there:
            groups += [part, across_cores(part)]
        return groups

    cot_mine, own, *other_widths = split(row_place, tokens, grad_out, row)
    stacked, cot_mine = stack(
        [own] + [shifted(part, "row", step + 1) for step, part in enumerate(other_widths)],
        cot_mine,
    )
    stacks = [stacked] + [shifted(stacked, "col", step) for step in range(1, col)]
    cots = [cot_mine] + [shifted(cot_mine, "col", step) for step in range(1, col)]
    w_first, w_second = load(place, w_in[:, 0, :], w_out[0], blocks, size, [stacked])
    places = jnp.concatenate([row_place, col_place])
    tok = tokens_in_order(places, stacks, row, [w_first])

    tok_other = [across_cores(x) for x in tok]
    cot = in_order(col_place, cots, [tok[0]])
    cot_other = across_cores(cot)
    cot_arrived = across_cores(mark([cot_other]))
    pre_total, pre_sent, tok_later = first(
        tok, tok_other, w_first, size, NN, "preact_partial", []
    )
    pre_parts = across_rows(pre_sent)
    back_total, back_sent, cot_later = first(
        [cot], [cot_other], w_second, size, NT, "back_partial", [pre_sent, cot_arrived]
    )
    back_parts = across_rows(back_sent)
    tok_there = [shifted(tok_later, "dp", CORES * b) for b in range(1, blocks)]
    cot_there = [shifted(cot_later, "dp", CORES * b) for b in range(1, blocks)]

    def col_total(own, sent):
        for step, part in enumerate(sent):
            own = own + shifted(part, "col", step + 1).astype(jnp.float32)
        return own.astype(jnp.bfloat16)

    out_keep, *rest = second(
        pre_total, pre_parts, None, w_second, size, "block_out_partial", [back_sent]
    )
    out_sends, (slopes, *hidden) = rest[:PIECES], rest[PIECES:]
    out_own, *out_sent = cores_sum(
        col_place, out_keep, [across_cores(x) for x in out_sends], col, "block_out_cores"
    )
    block_out = col_total(out_own, out_sent)
    tok_all = all_replicas(tok_later, tok_other, tok_there)
    cot_all = all_replicas(cot_later, [cot_other], cot_there)
    arrived = across_cores(mark(back_parts))
    in_keep, *rest = second(
        back_total, back_parts, slopes, w_first, size, "grad_in_partial", [out_own, tok_all[-1], arrived]
    )
    in_sends, grad_pre = rest[:PIECES], rest[PIECES:]
    in_own, *in_sent = cores_sum(
        col_place,
        in_keep,
        [across_cores(x) for x in in_sends],
        col,
        "grad_in_cores",
        [block_out, cot_all[-1]],
    )
    grad_in = col_total(in_own, in_sent)

    def to_owner(parts):
        return [parts[0]] + [shifted(parts[b], "dp", CORES * b) for b in range(1, blocks)]

    after = [in_own, block_out]
    grad_out_w = weight_grad(to_owner(hidden), cot_all, True, "grad_w_out", after)
    grad_in_w = weight_grad(tok_all, to_owner(grad_pre), False, "grad_w_in", after)
    return block_out, grad_in, grad_in_w[:, None, :], grad_out_w[None]


def solution(mesh):
    in_specs = (
        P(("dp", "row", "col"), None),
        P("row", "col", None),
        P("col", None, "row"),
        P(("dp", "col"), "row"),
    )
    out_specs = (
        P(("dp", "col"), "row"),
        P(("dp", "col"), "row"),
        P("row", "col", "dp"),
        P("col", "dp", "row"),
    )
    sizes = (mesh.shape["dp"], mesh.shape["row"], mesh.shape["col"])
    return jax.shard_map(
        functools.partial(body, *sizes),
        mesh=mesh,
        in_specs=in_specs,
        out_specs=out_specs,
        check_vma=False,
    )
```

```python
import functools

import jax
import jax.numpy as jnp
from jax import lax
from jax.experimental import pallas as pl
from jax.experimental.pallas import tpu as pltpu
from jax.sharding import PartitionSpec as P

CORES = 2
CFG = {'cot_early': 0, 'tok_pieces': 1, 'cot_pieces': 2, 'out_pieces': 2, 'in_pieces': 1, 'load2': 'pre', 'order2': 'load2', 'hop_cot': 0, 'hop_c': 0, 'hop_d': 0, 'back_pre': 0, 'tok_y': 'preact', 'cot_y': 'back', 'k3_back': 0, 'k3_toky': 0, 'se_d': 0, 'k4': ['E'], 'sf': ['bo'], 'wg_bo': 0, 'hid': 'merged'}
MIB = 1024 * 1024
NT = (((1,), (1,)), ((), ()))
NN = (((1,), (0,)), ((), ()))
TN = (((0,), (0,)), ((), ()))
VMEM = pl.BlockSpec(memory_space=pltpu.VMEM)
SMEM = pl.BlockSpec(memory_space=pltpu.SMEM)
HBM = pl.BlockSpec(memory_space=pltpu.HBM)
ANY = pl.BlockSpec(memory_space=pl.ANY)


def mm(a, b, dims):
    return lax.dot_general(a, b, dims, preferred_element_type=jnp.float32)


def tile_of(size, most):
    for tile in range(most, 0, -128):
        if size % tile == 0:
            return tile
    return size


def in_hbm(x):
    return pltpu.with_memory_space_constraint(x, pltpu.HBM)


def call(
    kernel, in_specs, out_specs, out_shape, name, scratch=(), limit=24, after=(), cost=0
):
    reads = len(in_specs)

    def run(*refs):
        kernel(*refs[:reads], *refs[reads + len(after) :])

    kernel_call = pl.pallas_call(
        run,
        in_specs=list(in_specs) + [ANY] * len(after),
        out_specs=out_specs,
        out_shape=out_shape,
        scratch_shapes=scratch,
        compiler_params=pltpu.CompilerParams(vmem_limit_bytes=limit * MIB),
        cost_estimate=pl.CostEstimate(flops=0, bytes_accessed=cost * MIB, transcendentals=0),
        name=name,
    )
    return lambda *args: kernel_call(*args, *after)


def shape(dims, dtype=jnp.bfloat16):
    return jax.ShapeDtypeStruct(tuple(dims), dtype)


def load_kernel(dp, size, pieces, columns, place, w, out, sems):
    blocks = dp // CORES
    rows = (w.shape[0] if columns else size) // pieces
    copies = []
    for b in range(blocks):
        for p in range(pieces):
            if columns:
                cut = pl.ds(p * rows, rows)
                source = w.at[cut, pl.ds(pl.multiple_of(lax.rem(place[0] + CORES * b, dp) * size, 128), size)]
                to = out.at[cut, pl.ds(b * size, size)]
            else:
                at = pl.multiple_of(lax.rem(place[0] + CORES * b, dp) * size + p * rows, 16)
                source = w.at[pl.ds(at, rows)]
                to = out.at[pl.ds(b * size + p * rows, rows)]
            copies.append(pltpu.make_async_copy(source, to, sems.at[b * pieces + p]))
    for copy in copies:
        copy.start()
    for copy in copies:
        copy.wait()


def load(place, w, dp, size, columns, name, after):
    blocks, pieces = dp // CORES, 8
    units = blocks * size
    return call(
        functools.partial(load_kernel, dp, size, pieces, columns),
        [SMEM, HBM],
        VMEM,
        pltpu.VMEM((w.shape[0], units) if columns else (units, w.shape[1]), jnp.bfloat16),
        name,
        scratch=[pltpu.SemaphoreType.DMA((blocks * pieces,))],
        after=after,
    )(place, in_hbm(w))


def split_kernel(place, tokens, cots, cot, *rest):
    *outs, sems = rest
    count, width = len(outs), outs[0].shape[1]
    copies = [pltpu.make_async_copy(cots, cot, sems.at[count])]
    for k in reversed(range(count)):
        at = lax.rem(place[0] + k, count) * width
        source = tokens.at[:, pl.ds(pl.multiple_of(at, 128), width)]
        copies.append(pltpu.make_async_copy(source, outs[k], sems.at[k]))
    for copy in reversed(copies):
        copy.start()
    for copy in copies:
        copy.wait()


def split(row_place, tokens, cots, count):
    rows, width = tokens.shape[0], tokens.shape[1] // count
    return call(
        split_kernel,
        [SMEM, HBM, HBM],
        [VMEM] * (1 + count),
        [shape(cots.shape)] + [shape((rows, width))] * count,
        "split_width",
        scratch=[pltpu.SemaphoreType.DMA((1 + count,))],
    )(row_place, tokens, cots)


def stack_kernel(*refs):
    *parts, cot, out, cot_out = refs
    out[...] = jnp.concatenate([r[...].astype(jnp.float32) for r in parts]).astype(out.dtype)
    cot_out[...] = cot[...]


def stack(parts, cot):
    rows, width = parts[0].shape
    return call(
        stack_kernel,
        [VMEM] * (1 + len(parts)),
        [VMEM] * 2,
        [shape((rows * len(parts), width)), shape(cot.shape)],
        "stack_rows",
    )(*parts, cot)


def tokens_kernel(row, pieces, row_place, col_place, *refs):
    stacks, outs, held = refs[: -1 - pieces], refs[-1 - pieces : -1], refs[-1]
    col, n = len(stacks), held.shape[1]
    rows_out = outs[0].shape[0]
    my_row, my_col = row_place[0], col_place[0]
    for k, part in enumerate(stacks):
        rows = part[...].astype(jnp.float32)
        for r in range(row):
            at = lax.rem(my_row + row - r, row) * col + lax.rem(my_col + col - k, col)
            held[at] = rows[r * n : (r + 1) * n]
    for at in range(0, row * col, 2):
        pair = jnp.concatenate([held[at], held[at + 1]])
        piece, start = divmod(at * n, rows_out)
        outs[piece][start : start + 2 * n] = pair.astype(jnp.bfloat16)


def tokens_in_order(row_place, col_place, stacks, row, after, pieces):
    rows, width = stacks[0].shape
    col = len(stacks)
    return call(
        functools.partial(tokens_kernel, row, pieces),
        [SMEM, SMEM] + [VMEM] * col,
        [VMEM] * pieces,
        [shape((rows * col // pieces, width))] * pieces,
        "order_tokens",
        scratch=[pltpu.VMEM((row * col, rows // row, width), jnp.float32)],
        after=after,
    )(row_place, col_place, *stacks)


def order_kernel(count, place, *refs):
    parts, outs, held = refs[:count], refs[count:-1], refs[-1]
    me, rows = place[0], parts[0].shape[0]
    for k, part in enumerate(parts):
        held[lax.rem(me + count - k, count)] = part[...]
    each = count // len(outs)
    for k in range(count):
        start = k % each * rows
        outs[k // each][start : start + rows] = held[k]


def in_order(col_place, parts, after, pieces):
    rows, width = parts[0].shape
    count = len(parts)
    return call(
        functools.partial(order_kernel, count),
        [SMEM] + [VMEM] * count,
        [VMEM] * pieces,
        [shape((rows * count // pieces, width))] * pieces,
        "order_rows",
        scratch=[pltpu.VMEM((count, rows, width), jnp.bfloat16)],
        after=after,
    )(col_place, *parts)


def first_kernel(dims, tile, mine, count, *refs):
    groups, w, refs = refs[:count], refs[count], refs[count + 1 :]
    if len(refs) == 6:
        refs[4][...] = refs[0][...]
        refs = refs[1:4] + refs[5:]
    total, sent, own_out, rows = refs
    at = 0
    for i, group in enumerate(groups):
        cut = slice(at, at + group.shape[0])
        rows[cut] = group[...]
        if i < mine:
            own_out[cut] = group[...]
        at += group.shape[0]
    for at in range(0, total.shape[1], tile):
        cut = slice(at, at + tile)
        part = mm(rows[...], w[:, cut] if dims is NN else w[cut, :], dims)
        total[:, cut] = part
        sent[:, cut] = part.astype(jnp.bfloat16)


def first(own, other, w, dims, name, after=(), passing=None):
    half, width = len(own) * own[0].shape[0], own[0].shape[1]
    n = 2 * half
    units = w.shape[1 if dims is NN else 0]
    extra = [] if passing is None else [passing]
    return call(
        functools.partial(first_kernel, dims, tile_of(units, 256), len(own), len(own) + len(other)),
        [VMEM] * (len(own) + len(other) + 1 + len(extra)),
        [VMEM] * (3 + len(extra)),
        [shape((n, units), jnp.float32), shape((n, units)), shape((half, width))]
        + [shape(x.shape) for x in extra],
        name,
        scratch=[pltpu.VMEM((n, width), jnp.bfloat16)],
        after=after,
    )(*own, *other, w, *extra)


def gelu_parts(preact):
    cdf = 0.5 * (1.0 + lax.erf(preact * 0.7071067811865476))
    slopes = cdf + preact * jnp.exp(-0.5 * preact * preact) * 0.3989422804014327
    return (preact * cdf, slopes)


def second_product(dims, vals, w, keep, sends):
    half, width = keep.shape
    tile = tile_of(width, 512)
    for at in range(0, width, tile):
        cut = slice(at, at + tile)
        part = mm(vals[...], w[:, cut] if dims is NN else w[cut, :], dims)
        keep[:, cut] = part[:half]
        for i, send in enumerate(sends):
            rows = send.shape[0]
            send[:, cut] = part[half + i * rows : half + (i + 1) * rows].astype(jnp.bfloat16)


def row_sum(total, parts, cut):
    whole = total[:, cut]
    for part in parts:
        whole = whole + part[:, cut].astype(jnp.float32)
    return whole


def forward_kernel(blocks, shares, pieces, passing, *refs):
    total, parts, w = refs[0], refs[1 : 1 + shares], refs[1 + shares]
    passed, refs = refs[2 + shares : 2 + shares + passing], refs[2 + shares + passing :]
    keep, *sends = refs[: 1 + pieces]
    slopes, *hidden, vals = refs[1 + pieces :]
    hidden, outs = hidden[:blocks], hidden[blocks:]
    for a, b in zip(passed, outs):
        b[...] = a[...]
    size = total.shape[1] // blocks
    for b in range(blocks):
        cut = slice(b * size, (b + 1) * size)
        value, slope = gelu_parts(row_sum(total, parts, cut))
        value = value.astype(jnp.bfloat16)
        vals[:, cut] = value
        hidden[b][...] = value
        slopes[:, cut] = slope
    second_product(NN, vals, w, keep, sends)


def backward_kernel(blocks, shares, pieces, passing, *refs):
    total, parts, slopes, w = refs[0], refs[1 : 1 + shares], refs[1 + shares], refs[2 + shares]
    hidden, refs = refs[3 + shares : 3 + shares + passing], refs[3 + shares + passing :]
    keep, *sends = refs[: 1 + pieces]
    *pre, vals = refs[1 + pieces :]
    n, size = total.shape[0], total.shape[1] // blocks
    for b in range(blocks):
        cut = slice(b * size, (b + 1) * size)
        value = (row_sum(total, parts, cut) * slopes[:, cut]).astype(jnp.bfloat16)
        vals[:, cut] = value
        pre[b][:n] = value
        if b > 0 and passing:
            pre[b][n:] = hidden[b - 1][...]
    second_product(NT, vals, w, keep, sends)


def second(total, parts, slopes, w, size, name, passing, after, pieces):
    n, units = total.shape
    half = n // 2
    blocks = units // size
    forward = slopes is None
    width = w.shape[1] if forward else w.shape[0]
    out_shape = [shape((half, width), jnp.float32)] + [shape((half // pieces, width))] * pieces
    if forward:
        out_shape.append(shape((n, units), jnp.float32))
        out_shape += [shape((n, size))] * blocks + [shape(x.shape) for x in passing]
    else:
        other = 2 * n if passing else n
        out_shape += [shape((n, size))] + [shape((other, size))] * (blocks - 1)
    extra = [] if forward else [slopes]
    kernel = forward_kernel if forward else backward_kernel
    return call(
        functools.partial(kernel, blocks, len(parts), pieces, len(passing)),
        [VMEM] * (2 + len(parts) + len(extra) + len(passing)),
        [VMEM] * len(out_shape),
        out_shape,
        name,
        scratch=[pltpu.VMEM((n, units), jnp.bfloat16)],
        after=after,
    )(total, *parts, *extra, w, *passing)


def cores_kernel(pieces, place, keep, *refs):
    parts, own = refs[:pieces], refs[pieces]
    *sent, held = refs[pieces + 1 :]
    rows = own.shape[0]
    at = 0
    for part in parts:
        cut = slice(at, at + part.shape[0])
        held[cut] = keep[cut] + part[...].astype(jnp.float32)
        at += part.shape[0]
    count = 1 + len(sent)
    me = place[0]
    for k in range(count):
        at = pl.ds(pl.multiple_of(lax.rem(me + k, count) * rows, 16), rows)
        if k == 0:
            own[...] = held[at]
        else:
            sent[k - 1][...] = held[at].astype(jnp.bfloat16)


def cores_sum(col_place, keep, parts, count, name, after=()):
    rows, width = keep.shape[0] // count, keep.shape[1]
    return call(
        functools.partial(cores_kernel, len(parts)),
        [SMEM, VMEM] + [VMEM] * len(parts),
        [VMEM] * count,
        [shape((rows, width), jnp.float32)] + [shape((rows, width))] * (count - 1),
        name,
        scratch=[pltpu.VMEM(keep.shape, jnp.float32)],
        after=after,
    )(col_place, keep, *parts)


def mark_kernel(*refs):
    refs[-1][...] = refs[0][:16, :128]


def mark(parts):
    return call(mark_kernel, [VMEM] * len(parts), VMEM, shape((16, 128)), "mark")(*parts)


def weight_kernel(left_cuts, right_cuts, tile, across, *refs):
    lefts = len(left_cuts)
    left, right, out = refs[:lefts], refs[lefts:-5], refs[-5]
    rows_left, rows_right, staged, sems = refs[-4:]
    for groups, cuts, rows in ((left, left_cuts, rows_left), (right, right_cuts, rows_right)):
        at = 0
        for group, (start, stop) in zip(groups, cuts):
            rows[at : at + stop - start] = group[start:stop]
            at += stop - start
    copies = []
    for i, at in enumerate(range(0, out.shape[1 if across else 0], tile)):
        cut = slice(at, at + tile)
        if across:
            part, where = mm(rows_left[...], rows_right[:, cut], TN), (slice(None), cut)
        else:
            part, where = mm(rows_left[:, cut], rows_right[...], TN), (cut, slice(None))
        staged[where] = part.astype(jnp.bfloat16)
        copies.append(pltpu.make_async_copy(staged.at[where], out.at[where], sems.at[i]))
        copies[-1].start()
    for copy in copies:
        copy.wait()


def weight_grad(left, right, across, name, after):
    left, left_cuts = [x for x, _ in left], [cut for _, cut in left]
    right, right_cuts = [x for x, _ in right], [cut for _, cut in right]
    n = sum(stop - start for start, stop in left_cuts)
    k, m = left[0].shape[1], right[0].shape[1]
    long = m if across else k
    tile = tile_of(long, 512)
    return call(
        functools.partial(weight_kernel, left_cuts, right_cuts, tile, across),
        [VMEM] * (len(left) + len(right)),
        HBM,
        shape((k, m)),
        name,
        scratch=[
            pltpu.VMEM((n, k), jnp.bfloat16),
            pltpu.VMEM((n, m), jnp.bfloat16),
            pltpu.VMEM((k, m), jnp.bfloat16),
            pltpu.SemaphoreType.DMA((long // tile,)),
        ],
        after=after,
        cost=0,
    )(*left, *right)


def body(dp, row, col, tokens, w_in, w_out, grad_out):
    blocks, m = dp // CORES, grad_out.shape[0]
    width, size = w_in.shape[0], w_in.shape[2] // dp
    mine = lax.axis_index("dp")
    place = mine.astype(jnp.int32)[None]
    row_place = lax.axis_index("row").astype(jnp.int32)[None]
    col_place = lax.axis_index("col").astype(jnp.int32)[None]
    C = CFG

    def shifted(x, axis, step):
        count = {"dp": dp, "row": row, "col": col}[axis]
        return lax.ppermute(x, axis, [(i, (i + step) % count) for i in range(count)])

    def across_cores(x):
        return lax.ppermute(x, "dp", [(i, i ^ 1) for i in range(dp)])

    def across_rows(x):
        return [shifted(x, "row", step) for step in range(1, row)]

    def all_replicas(own, other, there):
        groups = [own, *other]
        for part in there:
            groups += [part, across_cores(part)]
        return groups

    def hop(parts, on):
        return [across_cores(mark(parts))] if on else []

    cot_mine, own, *other_widths = split(row_place, in_hbm(tokens), in_hbm(grad_out), row)
    stacked, cot_mine2 = stack(
        [own] + [shifted(part, "row", step + 1) for step, part in enumerate(other_widths)],
        cot_mine,
    )
    src = cot_mine if C["cot_early"] else cot_mine2
    stacks = [stacked] + [shifted(stacked, "col", step) for step in range(1, col)]
    cots = [src] + [shifted(src, "col", step) for step in range(1, col)]
    w_first = load(place, w_in[:, 0, :], dp, size, True, "load_first", [stacked])
    tok = tokens_in_order(row_place, col_place, stacks, row, [w_first], C["tok_pieces"])
    tok_other = [across_cores(x) for x in tok]
    pre_total, pre_sent, tok_later = first(tok, tok_other, w_first, NN, "preact_partial")
    pre_parts = across_rows(pre_sent)
    w_second = load(place, w_out[0], dp, size, False, "load_second", {"first": [w_first], "tok": [tok[0]], "pre": [pre_sent]}[C["load2"]])
    cot = in_order(col_place, cots, {"first": [w_first], "tok": [tok[0]], "pre": [pre_sent], "load2": [w_second]}[C["order2"]], C["cot_pieces"])
    cot_other = [across_cores(x) for x in cot]
    hops = hop(cot_other, C["hop_cot"])
    back_total, back_sent, cot_later, *passed = first(cot, cot_other, w_second, NT, "back_partial", [pre_sent] * C["back_pre"] + hops, tok_later if C["tok_y"] == "back" else None)
    if passed:
        tok_later = passed[0]
    back_parts = across_rows(back_sent)
    if C["tok_y"] != "K3":
        tok_there = [shifted(tok_later, "dp", CORES * b) for b in range(1, blocks)]
    if C["cot_y"] != "K3":
        cot_there = [shifted(cot_later, "dp", CORES * b) for b in range(1, blocks)]
    after = [back_sent] * C["k3_back"] + (tok_there if C["k3_toky"] else [])
    after += hop(pre_parts, C["hop_c"])
    passing = [tok_later] * (C["tok_y"] == "K3") + [cot_later] * (C["cot_y"] == "K3")
    out_keep, *rest = second(
        pre_total, pre_parts, None, w_second, size, "block_out_partial", passing, after, C["out_pieces"]
    )
    out_sends, rest = rest[: C["out_pieces"]], rest[C["out_pieces"] :]
    slopes, rest = rest[0], rest[1:]
    hidden, passed = rest[:blocks], rest[blocks:]
    if C["tok_y"] == "K3":
        tok_there = [shifted(passed[0], "dp", CORES * b) for b in range(1, blocks)]
    if C["cot_y"] == "K3":
        cot_there = [shifted(passed[-1], "dp", CORES * b) for b in range(1, blocks)]
    out_own, *out_sent = cores_sum(
        col_place, out_keep, [across_cores(x) for x in out_sends], col, "block_out_cores",
        back_parts if C["se_d"] else []
    )

    def col_total(own, sent):
        for step, part in enumerate(sent):
            own = own + shifted(part, "col", step + 1).astype(jnp.float32)
        return own.astype(jnp.bfloat16)

    block_out = col_total(out_own, out_sent)
    tok_all = all_replicas(tok_later, tok_other, tok_there)
    cot_all = all_replicas(cot_later, cot_other, cot_there)
    full_ties = {"E": out_own, "bo": block_out, "ty": tok_there[-1], "cy": cot_there[-1], "tx": tok_all[-1], "cx": cot_all[-1]}
    after = [full_ties[t] for t in C["k4"]] + hop(back_parts, C["hop_d"])
    merged = C["hid"] == "merged"
    in_keep, *rest = second(
        back_total, back_parts, slopes, w_first, size, "grad_in_partial", hidden[1:] if merged else (), after, C["in_pieces"]
    )
    in_sends, both = rest[: C["in_pieces"]], rest[C["in_pieces"] :]
    in_own, *in_sent = cores_sum(
        col_place, in_keep, [across_cores(x) for x in in_sends], col, "grad_in_cores",
        [full_ties[t] for t in C["sf"]]
    )
    grad_in = col_total(in_own, in_sent)

    def full(groups):
        return [(x, (0, x.shape[0])) for x in groups]

    owned = [shifted(both[b], "dp", CORES * b) for b in range(1, blocks)]
    n = hidden[0].shape[0]
    pre_mine = full(both[:1]) + [(x, (0, n)) for x in owned]
    if merged:
        hid_mine = full(hidden[:1]) + [(x, (n, 2 * n)) for x in owned]
    else:
        hid_mine = full(hidden[:1] + [shifted(hidden[b], "dp", CORES * b) for b in range(1, blocks)])
    after = [in_own] + [block_out] * C["wg_bo"]
    grad_out_w = weight_grad(hid_mine, full(cot_all), True, "grad_w_out", after)
    grad_in_w = weight_grad(full(tok_all), pre_mine, False, "grad_w_in", after)
    return block_out, grad_in, grad_in_w[:, None, :], grad_out_w[None]


def solution(mesh):
    in_specs = (
        P(("dp", "row", "col"), None),
        P("row", "col", None),
        P("col", None, "row"),
        P(("dp", "col"), "row"),
    )
    out_specs = (
        P(("dp", "col"), "row"),
        P(("dp", "col"), "row"),
        P("row", "col", "dp"),
        P("col", "dp", "row"),
    )
    sizes = (mesh.shape["dp"], mesh.shape["row"], mesh.shape["col"])
    return jax.shard_map(
        functools.partial(body, *sizes),
        mesh=mesh,
        in_specs=in_specs,
        out_specs=out_specs,
        check_vma=False,
    )
```

```python
import functools

import jax
import jax.numpy as jnp
from jax import lax
from jax.experimental import pallas as pl
from jax.experimental.pallas import tpu as pltpu
from jax.sharding import PartitionSpec as P

CORES = 2
CFG = {'cot_early': 0, 'tok_pieces': 1, 'cot_pieces': 2, 'out_pieces': 2, 'in_pieces': 1, 'load2': 'pre', 'order2': 'load2', 'hop_cot': 0, 'hop_c': 0, 'hop_d': 0, 'back_pre': 0, 'tok_y': 'preact', 'cot_y': 'back', 'k3_back': 1, 'k3_toky': 0, 'se_d': 0, 'k4': ['E', 'ty'], 'sf': ['bo', 'cy'], 'wg_bo': 0, 'hid': 'sep', 'wgo': 'SF', 'half': 0, 'sfs': []}
MIB = 1024 * 1024
NT = (((1,), (1,)), ((), ()))
NN = (((1,), (0,)), ((), ()))
TN = (((0,), (0,)), ((), ()))
VMEM = pl.BlockSpec(memory_space=pltpu.VMEM)
SMEM = pl.BlockSpec(memory_space=pltpu.SMEM)
HBM = pl.BlockSpec(memory_space=pltpu.HBM)
ANY = pl.BlockSpec(memory_space=pl.ANY)


def mm(a, b, dims):
    return lax.dot_general(a, b, dims, preferred_element_type=jnp.float32)


def mm_streamed(rows, weights):
    return mm(weights, rows, NT).T


def tile_of(size, most):
    for tile in range(most, 0, -128):
        if size % tile == 0:
            return tile
    return size


def in_hbm(x):
    return pltpu.with_memory_space_constraint(x, pltpu.HBM)


def call(
    kernel, in_specs, out_specs, out_shape, name, scratch=(), limit=24, after=(), cost=0
):
    reads = len(in_specs)

    def run(*refs):
        kernel(*refs[:reads], *refs[reads + len(after) :])

    kernel_call = pl.pallas_call(
        run,
        in_specs=list(in_specs) + [ANY] * len(after),
        out_specs=out_specs,
        out_shape=out_shape,
        scratch_shapes=scratch,
        compiler_params=pltpu.CompilerParams(vmem_limit_bytes=limit * MIB),
        cost_estimate=pl.CostEstimate(flops=0, bytes_accessed=cost * MIB, transcendentals=0),
        name=name,
    )
    return lambda *args: kernel_call(*args, *after)


def shape(dims, dtype=jnp.bfloat16):
    return jax.ShapeDtypeStruct(tuple(dims), dtype)


def load_kernel(dp, size, pieces, columns, which, place, w, out, sems):
    rows = (w.shape[0] if columns else size) // pieces
    copies = []
    for i, b in enumerate(which):
        for p in range(pieces):
            if columns:
                cut = pl.ds(p * rows, rows)
                source = w.at[cut, pl.ds(pl.multiple_of(lax.rem(place[0] + CORES * b, dp) * size, 128), size)]
                to = out.at[cut, pl.ds(i * size, size)]
            else:
                at = pl.multiple_of(lax.rem(place[0] + CORES * b, dp) * size + p * rows, 16)
                source = w.at[pl.ds(at, rows)]
                to = out.at[pl.ds(i * size + p * rows, rows)]
            copies.append(pltpu.make_async_copy(source, to, sems.at[i * pieces + p]))
    for copy in copies:
        copy.start()
    for copy in copies:
        copy.wait()


def load(place, w, dp, size, columns, which, name, after):
    blocks, pieces = len(which), 4
    units = blocks * size
    return call(
        functools.partial(load_kernel, dp, size, pieces, columns, which),
        [SMEM, HBM],
        VMEM,
        pltpu.VMEM((w.shape[0], units) if columns else (units, w.shape[1]), jnp.bfloat16),
        name,
        scratch=[pltpu.SemaphoreType.DMA((blocks * pieces,))],
        after=after,
    )(place, in_hbm(w))


def split_kernel(place, tokens, cots, cot, *rest):
    *outs, sems = rest
    count, width = len(outs), outs[0].shape[1]
    copies = [pltpu.make_async_copy(cots, cot, sems.at[count])]
    for k in reversed(range(count)):
        at = lax.rem(place[0] + k, count) * width
        source = tokens.at[:, pl.ds(pl.multiple_of(at, 128), width)]
        copies.append(pltpu.make_async_copy(source, outs[k], sems.at[k]))
    for copy in reversed(copies):
        copy.start()
    for copy in copies:
        copy.wait()


def split(row_place, tokens, cots, count):
    rows, width = tokens.shape[0], tokens.shape[1] // count
    return call(
        split_kernel,
        [SMEM, HBM, HBM],
        [VMEM] * (1 + count),
        [shape(cots.shape)] + [shape((rows, width))] * count,
        "split_width",
        scratch=[pltpu.SemaphoreType.DMA((1 + count,))],
    )(row_place, tokens, cots)


def stack_kernel(*refs):
    *parts, cot, out, cot_out = refs
    out[...] = jnp.concatenate([r[...].astype(jnp.float32) for r in parts]).astype(out.dtype)
    cot_out[...] = cot[...]


def stack(parts, cot, after):
    rows, width = parts[0].shape
    return call(
        stack_kernel,
        [VMEM] * (1 + len(parts)),
        [VMEM] * 2,
        [shape((rows * len(parts), width)), shape(cot.shape)],
        "stack_rows",
        after=after,
    )(*parts, cot)


def tokens_kernel(row, pieces, row_place, col_place, *refs):
    stacks, outs, held = refs[: -1 - pieces], refs[-1 - pieces : -1], refs[-1]
    col, n = len(stacks), held.shape[1]
    rows_out = outs[0].shape[0]
    my_row, my_col = row_place[0], col_place[0]
    for k, part in enumerate(stacks):
        rows = part[...].astype(jnp.float32)
        for r in range(row):
            at = lax.rem(my_row + row - r, row) * col + lax.rem(my_col + col - k, col)
            held[at] = rows[r * n : (r + 1) * n]
    for at in range(0, row * col, 2):
        pair = jnp.concatenate([held[at], held[at + 1]])
        piece, start = divmod(at * n, rows_out)
        outs[piece][start : start + 2 * n] = pair.astype(jnp.bfloat16)


def tokens_in_order(row_place, col_place, stacks, row, after, pieces):
    rows, width = stacks[0].shape
    col = len(stacks)
    return call(
        functools.partial(tokens_kernel, row, pieces),
        [SMEM, SMEM] + [VMEM] * col,
        [VMEM] * pieces,
        [shape((rows * col // pieces, width))] * pieces,
        "order_tokens",
        scratch=[pltpu.VMEM((row * col, rows // row, width), jnp.float32)],
        after=after,
    )(row_place, col_place, *stacks)


def order_kernel(count, place, *refs):
    parts, outs, held = refs[:count], refs[count:-1], refs[-1]
    me, rows = place[0], parts[0].shape[0]
    for k, part in enumerate(parts):
        held[lax.rem(me + count - k, count)] = part[...]
    each = count // len(outs)
    for k in range(count):
        start = k % each * rows
        outs[k // each][start : start + rows] = held[k]


def in_order(col_place, parts, after, pieces):
    rows, width = parts[0].shape
    count = len(parts)
    return call(
        functools.partial(order_kernel, count),
        [SMEM] + [VMEM] * count,
        [VMEM] * pieces,
        [shape((rows * count // pieces, width))] * pieces,
        "order_rows",
        scratch=[pltpu.VMEM((count, rows, width), jnp.bfloat16)],
        after=after,
    )(col_place, *parts)


def first_kernel(dims, tile, mine, count, weights, *refs):
    groups, ws, refs = refs[:count], refs[count : count + weights], refs[count + weights :]
    if len(refs) == 6:
        refs[4][...] = refs[0][...]
        refs = refs[1:4] + refs[5:]
    total, sent, own_out, rows = refs
    at = 0
    for i, group in enumerate(groups):
        cut = slice(at, at + group.shape[0])
        rows[cut] = group[...]
        if i < mine:
            own_out[cut] = group[...]
        at += group.shape[0]
    size = total.shape[1] // weights
    for at in range(0, total.shape[1], tile):
        cut = slice(at, at + tile)
        b, start = divmod(at, size)
        units = slice(start, start + tile)
        if dims is NN:
            part = mm(rows[...], ws[b][:, units], NN)
        else:
            part = mm_streamed(rows[...], ws[b][units, :])
        total[:, cut] = part
        sent[:, cut] = part.astype(jnp.bfloat16)


def first(own, other, ws, dims, name, after=(), passing=None):
    half, width = len(own) * own[0].shape[0], own[0].shape[1]
    n = 2 * half
    each = ws[0].shape[1 if dims is NN else 0]
    units = len(ws) * each
    extra = [] if passing is None else [passing]
    return call(
        functools.partial(
            first_kernel,
            dims,
            tile_of(each, 256 if dims is NN else 512),
            len(own),
            len(own) + len(other),
            len(ws),
        ),
        [VMEM] * (len(own) + len(other) + len(ws) + len(extra)),
        [VMEM] * (3 + len(extra)),
        [shape((n, units), jnp.float32), shape((n, units)), shape((half, width))]
        + [shape(x.shape) for x in extra],
        name,
        scratch=[pltpu.VMEM((n, width), jnp.bfloat16)],
        after=after,
    )(*own, *other, *ws, *extra)


def gelu_parts(preact):
    cdf = 0.5 * (1.0 + lax.erf(preact * 0.7071067811865476))
    slopes = cdf + preact * jnp.exp(-0.5 * preact * preact) * 0.3989422804014327
    return (preact * cdf, slopes)


def second_product(dims, vals, ws, keep, sends):
    half, width = keep.shape
    tile = tile_of(width, 512)
    for at in range(0, width, tile):
        cut = slice(at, at + tile)
        if dims is NN:
            size = vals.shape[1] // len(ws)
            part = mm(vals[:, :size], ws[0][:, cut], NN)
            for b in range(1, len(ws)):
                part += mm(vals[:, b * size : (b + 1) * size], ws[b][:, cut], NN)
        else:
            part = mm_streamed(vals[...], ws[0][cut, :])
        keep[:, cut] = part[:half]
        for i, send in enumerate(sends):
            rows = send.shape[0]
            send[:, cut] = part[half + i * rows : half + (i + 1) * rows].astype(jnp.bfloat16)


def row_sum(total, parts, cut):
    whole = total[:, cut]
    for part in parts:
        whole = whole + part[:, cut].astype(jnp.float32)
    return whole


def forward_kernel(blocks, shares, pieces, passing, weights, *refs):
    total, parts, refs = refs[0], refs[1 : 1 + shares], refs[1 + shares :]
    ws, refs = refs[:weights], refs[weights:]
    passed, refs = refs[:passing], refs[passing:]
    keep, *sends = refs[: 1 + pieces]
    slopes, *hidden, vals = refs[1 + pieces :]
    hidden, outs = hidden[:blocks], hidden[blocks:]
    for a, b in zip(passed, outs):
        b[...] = a[...]
    size = total.shape[1] // blocks
    for b in range(blocks):
        cut = slice(b * size, (b + 1) * size)
        value, slope = gelu_parts(row_sum(total, parts, cut))
        value = value.astype(jnp.bfloat16)
        vals[:, cut] = value
        hidden[b][...] = value
        slopes[:, cut] = slope
    second_product(NN, vals, ws, keep, sends)


def backward_kernel(blocks, shares, pieces, passing, weights, *refs):
    total, parts, slopes, w = refs[0], refs[1 : 1 + shares], refs[1 + shares], refs[2 + shares]
    hidden, refs = refs[3 + shares : 3 + shares + passing], refs[3 + shares + passing :]
    keep, *sends = refs[: 1 + pieces]
    *pre, vals = refs[1 + pieces :]
    n, size = total.shape[0], total.shape[1] // blocks
    for b in range(blocks):
        cut = slice(b * size, (b + 1) * size)
        value = (row_sum(total, parts, cut) * slopes[:, cut]).astype(jnp.bfloat16)
        vals[:, cut] = value
        pre[b][:n] = value
        if b > 0 and passing:
            pre[b][n:] = hidden[b - 1][...]
    second_product(NT, vals, [w], keep, sends)


def second(total, parts, slopes, ws, size, name, passing, after, pieces):
    n, units = total.shape
    half = n // 2
    blocks = units // size
    forward = slopes is None
    width = ws[0].shape[1] if forward else ws[0].shape[0]
    out_shape = [shape((half, width), jnp.float32)] + [shape((half // pieces, width))] * pieces
    if forward:
        out_shape.append(shape((n, units), jnp.float32))
        out_shape += [shape((n, size))] * blocks + [shape(x.shape) for x in passing]
    else:
        other = 2 * n if passing else n
        out_shape += [shape((n, size))] + [shape((other, size))] * (blocks - 1)
    extra = [] if forward else [slopes]
    kernel = forward_kernel if forward else backward_kernel
    return call(
        functools.partial(kernel, blocks, len(parts), pieces, len(passing), len(ws)),
        [VMEM] * (1 + len(parts) + len(extra) + len(ws) + len(passing)),
        [VMEM] * len(out_shape),
        out_shape,
        name,
        scratch=[pltpu.VMEM((n, units), jnp.bfloat16)],
        after=after,
    )(total, *parts, *extra, *ws, *passing)


def cores_kernel(pieces, count, steps, place, keep, *refs):
    parts, outs, held = refs[:pieces], refs[pieces:-1], refs[-1]
    rows = keep.shape[0] // count
    at = 0
    for part in parts:
        cut = slice(at, at + part.shape[0])
        held[cut] = keep[cut] + part[...].astype(jnp.float32)
        at += part.shape[0]
    for k, out in zip(steps, outs):
        at = pl.ds(pl.multiple_of(lax.rem(place[0] + k, count) * rows, 16), rows)
        out[...] = held[at].astype(out.dtype)


def cores_sum(col_place, keep, parts, count, steps, name, after=()):
    rows, width = keep.shape[0] // count, keep.shape[1]
    return call(
        functools.partial(cores_kernel, len(parts), count, steps),
        [SMEM, VMEM] + [VMEM] * len(parts),
        [VMEM] * len(steps),
        [shape((rows, width), jnp.bfloat16 if k else jnp.float32) for k in steps],
        name,
        scratch=[pltpu.VMEM(keep.shape, jnp.float32)],
        after=after,
    )(col_place, keep, *parts)


def mark_kernel(*refs):
    refs[-1][...] = refs[0][:16, :128]


def mark(parts):
    return call(mark_kernel, [VMEM] * len(parts), VMEM, shape((16, 128)), "mark")(*parts)


def weight_kernel(left_cuts, right_cuts, tile, across, *refs):
    lefts = len(left_cuts)
    left, right, out = refs[:lefts], refs[lefts:-5], refs[-5]
    rows_left, rows_right, staged, sems = refs[-4:]
    for groups, cuts, rows in ((left, left_cuts, rows_left), (right, right_cuts, rows_right)):
        at = 0
        for group, (start, stop) in zip(groups, cuts):
            rows[at : at + stop - start] = group[start:stop]
            at += stop - start
    copies = []
    for i, at in enumerate(range(0, out.shape[1 if across else 0], tile)):
        cut = slice(at, at + tile)
        if across:
            part, where = mm(rows_left[...], rows_right[:, cut], TN), (slice(None), cut)
        else:
            part, where = mm(rows_left[:, cut], rows_right[...], TN), (cut, slice(None))
        staged[where] = part.astype(jnp.bfloat16)
        copies.append(pltpu.make_async_copy(staged.at[where], out.at[where], sems.at[i]))
        copies[-1].start()
    for copy in copies:
        copy.wait()


def weight_grad(left, right, across, name, after):
    left, left_cuts = [x for x, _ in left], [cut for _, cut in left]
    right, right_cuts = [x for x, _ in right], [cut for _, cut in right]
    n = sum(stop - start for start, stop in left_cuts)
    k, m = left[0].shape[1], right[0].shape[1]
    long = m if across else k
    tile = tile_of(long, 512)
    return call(
        functools.partial(weight_kernel, left_cuts, right_cuts, tile, across),
        [VMEM] * (len(left) + len(right)),
        HBM,
        shape((k, m)),
        name,
        scratch=[
            pltpu.VMEM((n, k), jnp.bfloat16),
            pltpu.VMEM((n, m), jnp.bfloat16),
            pltpu.VMEM((k, m), jnp.bfloat16),
            pltpu.SemaphoreType.DMA((long // tile,)),
        ],
        after=after,
        cost=0,
    )(*left, *right)


def body(dp, row, col, tokens, w_in, w_out, grad_out):
    blocks, m = dp // CORES, grad_out.shape[0]
    width, size = w_in.shape[0], w_in.shape[2] // dp
    mine = lax.axis_index("dp")
    place = mine.astype(jnp.int32)[None]
    row_place = lax.axis_index("row").astype(jnp.int32)[None]
    col_place = lax.axis_index("col").astype(jnp.int32)[None]
    C = CFG

    def shifted(x, axis, step):
        count = {"dp": dp, "row": row, "col": col}[axis]
        return lax.ppermute(x, axis, [(i, (i + step) % count) for i in range(count)])

    def across_cores(x):
        return lax.ppermute(x, "dp", [(i, i ^ 1) for i in range(dp)])

    def across_rows(x):
        return [shifted(x, "row", step) for step in range(1, row)]

    def all_replicas(own, other, there):
        groups = [own, *other]
        for part in there:
            groups += [part, across_cores(part)]
        return groups

    def hop(parts, on):
        return [across_cores(mark(parts))] if on else []

    cot_mine, own, *other_widths = split(row_place, in_hbm(tokens), in_hbm(grad_out), row)
    w_begin = None
    if C["half"]:
        w_begin = load(place, w_out[0], dp, size, False, range(1), "load_half", [own])
    stacked, cot_mine2 = stack(
        [own] + [shifted(part, "row", step + 1) for step, part in enumerate(other_widths)],
        cot_mine,
        [w_begin] if C["half"] else [],
    )
    src = cot_mine if C["cot_early"] else cot_mine2
    stacks = [stacked] + [shifted(stacked, "col", step) for step in range(1, col)]
    cots = [src] + [shifted(src, "col", step) for step in range(1, col)]
    w_first = load(place, w_in[:, 0, :], dp, size, True, range(blocks), "load_first", [stacked])
    tok = tokens_in_order(row_place, col_place, stacks, row, [w_first], C["tok_pieces"])
    tok_other = [across_cores(x) for x in tok]
    pre_total, pre_sent, tok_later = first(tok, tok_other, [w_first], NN, "preact_partial")
    pre_parts = across_rows(pre_sent)
    w_rest = load(place, w_out[0], dp, size, False, range(C["half"], blocks), "load_half" if C["half"] else "load_second", {"first": [w_first], "tok": [tok[0]], "pre": [pre_sent]}[C["load2"]])
    w_second = ([w_begin] if C["half"] else []) + [w_rest]
    cot = in_order(col_place, cots, {"first": [w_first], "tok": [tok[0]], "pre": [pre_sent], "load2": [w_rest]}[C["order2"]], C["cot_pieces"])
    cot_other = [across_cores(x) for x in cot]
    hops = hop(cot_other, C["hop_cot"])
    back_total, back_sent, cot_later, *passed = first(cot, cot_other, w_second, NT, "back_partial", [pre_sent] * C["back_pre"] + hops, tok_later if C["tok_y"] == "back" else None)
    if passed:
        tok_later = passed[0]
    back_parts = across_rows(back_sent)
    if C["tok_y"] != "K3":
        tok_there = [shifted(tok_later, "dp", CORES * b) for b in range(1, blocks)]
    if C["cot_y"] != "K3":
        cot_there = [shifted(cot_later, "dp", CORES * b) for b in range(1, blocks)]
    after = [back_sent] * C["k3_back"] + (tok_there if C["k3_toky"] else [])
    after += hop(pre_parts, C["hop_c"])
    passing = [tok_later] * (C["tok_y"] == "K3") + [cot_later] * (C["cot_y"] == "K3")
    out_keep, *rest = second(
        pre_total, pre_parts, None, w_second, size, "block_out_partial", passing, after, C["out_pieces"]
    )
    out_sends, rest = rest[: C["out_pieces"]], rest[C["out_pieces"] :]
    slopes, rest = rest[0], rest[1:]
    hidden, passed = rest[:blocks], rest[blocks:]
    if C["tok_y"] == "K3":
        tok_there = [shifted(passed[0], "dp", CORES * b) for b in range(1, blocks)]
    if C["cot_y"] == "K3":
        cot_there = [shifted(passed[-1], "dp", CORES * b) for b in range(1, blocks)]
    out_own, *out_sent = cores_sum(
        col_place, out_keep, [across_cores(x) for x in out_sends], col, range(col), "block_out_cores",
        back_parts if C["se_d"] else []
    )

    def col_total(own, sent):
        for step, part in enumerate(sent):
            own = own + shifted(part, "col", step + 1).astype(jnp.float32)
        return own.astype(jnp.bfloat16)

    block_out = col_total(out_own, out_sent)
    tok_all = all_replicas(tok_later, tok_other, tok_there)
    cot_all = all_replicas(cot_later, cot_other, cot_there)
    full_ties = {"E": out_own, "bo": block_out, "ty": tok_there[-1], "cy": cot_there[-1], "tx": tok_all[-1], "cx": cot_all[-1]}
    after = [full_ties[t] for t in C["k4"]] + hop(back_parts, C["hop_d"])
    merged = C["hid"] == "merged"
    in_keep, *rest = second(
        back_total, back_parts, slopes, [w_first], size, "grad_in_partial", hidden[1:] if merged else (), after, C["in_pieces"]
    )
    in_sends, both = rest[: C["in_pieces"]], rest[C["in_pieces"] :]
    in_parts = [across_cores(x) for x in in_sends]
    ahead = [k for k in C["sfs"] if k < col]
    late = [k for k in range(col) if k not in ahead]
    sums = {}
    if ahead:
        sums.update(zip(ahead, cores_sum(col_place, in_keep, in_parts, col, ahead, "grad_in_ahead")))
    ties = [full_ties[t] for t in C["sf"]]
    sums.update(zip(late, cores_sum(col_place, in_keep, in_parts, col, late, "grad_in_cores", ties)))
    in_own = sums[0]
    grad_in = col_total(in_own, [sums[k] for k in range(1, col)])

    def full(groups):
        return [(x, (0, x.shape[0])) for x in groups]

    owned = [shifted(both[b], "dp", CORES * b) for b in range(1, blocks)]
    n = hidden[0].shape[0]
    pre_mine = full(both[:1]) + [(x, (0, n)) for x in owned]
    if merged:
        hid_mine = full(hidden[:1]) + [(x, (n, 2 * n)) for x in owned]
    else:
        hid_mine = full(hidden[:1] + [shifted(hidden[b], "dp", CORES * b) for b in range(1, blocks)])
    after = [in_own] + [block_out] * C["wg_bo"]
    out_after = {"none": [], "E": [out_own], "K4": [in_keep], "SF": after}[C["wgo"]]
    grad_out_w = weight_grad(hid_mine, full(cot_all), True, "grad_w_out", out_after)
    grad_in_w = weight_grad(full(tok_all), pre_mine, False, "grad_w_in", after)
    return block_out, grad_in, grad_in_w[:, None, :], grad_out_w[None]


def solution(mesh):
    in_specs = (
        P(("dp", "row", "col"), None),
        P("row", "col", None),
        P("col", None, "row"),
        P(("dp", "col"), "row"),
    )
    out_specs = (
        P(("dp", "col"), "row"),
        P(("dp", "col"), "row"),
        P("row", "col", "dp"),
        P("col", "dp", "row"),
    )
    sizes = (mesh.shape["dp"], mesh.shape["row"], mesh.shape["col"])
    return jax.shard_map(
        functools.partial(body, *sizes),
        mesh=mesh,
        in_specs=in_specs,
        out_specs=out_specs,
        check_vma=False,
    )
```

```python
import functools

import jax
import jax.numpy as jnp
from jax import lax
from jax.experimental import pallas as pl
from jax.experimental.pallas import tpu as pltpu
from jax.sharding import PartitionSpec as P

CORES = 2
OUT_PIECES = 2
COT_PIECES = 2
VMEM_LIMIT = 24 * 1024 * 1024
NT = (((1,), (1,)), ((), ()))
NN = (((1,), (0,)), ((), ()))
TN = (((0,), (0,)), ((), ()))
VMEM = pl.BlockSpec(memory_space=pltpu.VMEM)
SMEM = pl.BlockSpec(memory_space=pltpu.SMEM)
HBM = pl.BlockSpec(memory_space=pltpu.HBM)
ANY = pl.BlockSpec(memory_space=pl.ANY)


def mm(a, b, dims):
    return lax.dot_general(a, b, dims, preferred_element_type=jnp.float32)


def mm_streamed(rows, weights):
    return mm(weights, rows, NT).T


def tile_of(size, most):
    for tile in range(most, 0, -128):
        if size % tile == 0:
            return tile
    return size


def in_hbm(x):
    return pltpu.with_memory_space_constraint(x, pltpu.HBM)


def call(kernel, in_specs, out_specs, out_shape, name, scratch=(), after=()):
    reads = len(in_specs)

    def run(*refs):
        kernel(*refs[:reads], *refs[reads + len(after) :])

    kernel_call = pl.pallas_call(
        run,
        in_specs=list(in_specs) + [ANY] * len(after),
        out_specs=out_specs,
        out_shape=out_shape,
        scratch_shapes=scratch,
        compiler_params=pltpu.CompilerParams(vmem_limit_bytes=VMEM_LIMIT),
        cost_estimate=pl.CostEstimate(flops=0, bytes_accessed=0, transcendentals=0),
        name=name,
    )
    return lambda *args: kernel_call(*args, *after)


def shape(dims, dtype=jnp.bfloat16):
    return jax.ShapeDtypeStruct(tuple(dims), dtype)


def load_kernel(dp, size, pieces, columns, place, w, out, sems):
    rows = (w.shape[0] if columns else size) // pieces
    copies = []
    for b in range(dp // CORES):
        start = lax.rem(place[0] + CORES * b, dp) * size
        for p in range(pieces):
            if columns:
                cut = pl.ds(p * rows, rows)
                source = w.at[cut, pl.ds(pl.multiple_of(start, 128), size)]
                to = out.at[cut, pl.ds(b * size, size)]
            else:
                source = w.at[pl.ds(pl.multiple_of(start + p * rows, 16), rows)]
                to = out.at[pl.ds(b * size + p * rows, rows)]
            copies.append(pltpu.make_async_copy(source, to, sems.at[b * pieces + p]))
    for copy in copies:
        copy.start()
    for copy in copies:
        copy.wait()


def load(place, w, dp, size, columns, name, after):
    blocks, pieces = dp // CORES, 4
    units = blocks * size
    return call(
        functools.partial(load_kernel, dp, size, pieces, columns),
        [SMEM, HBM],
        VMEM,
        pltpu.VMEM((w.shape[0], units) if columns else (units, w.shape[1]), jnp.bfloat16),
        name,
        scratch=[pltpu.SemaphoreType.DMA((blocks * pieces,))],
        after=after,
    )(place, in_hbm(w))


def split_kernel(place, tokens, cots, cot, *rest):
    *outs, sems = rest
    count, width = len(outs), outs[0].shape[1]
    copies = [pltpu.make_async_copy(cots, cot, sems.at[count])]
    for k in reversed(range(count)):
        at = lax.rem(place[0] + k, count) * width
        source = tokens.at[:, pl.ds(pl.multiple_of(at, 128), width)]
        copies.append(pltpu.make_async_copy(source, outs[k], sems.at[k]))
    for copy in reversed(copies):
        copy.start()
    for copy in copies:
        copy.wait()


def split(row_place, tokens, cots, count):
    rows, width = tokens.shape[0], tokens.shape[1] // count
    return call(
        split_kernel,
        [SMEM, HBM, HBM],
        [VMEM] * (1 + count),
        [shape(cots.shape)] + [shape((rows, width))] * count,
        "split_width",
        scratch=[pltpu.SemaphoreType.DMA((1 + count,))],
    )(row_place, tokens, cots)


def stack_kernel(*refs):
    *parts, cot, out, cot_out = refs
    out[...] = jnp.concatenate([r[...].astype(jnp.float32) for r in parts]).astype(out.dtype)
    cot_out[...] = cot[...]


def stack(parts, cot):
    rows, width = parts[0].shape
    return call(
        stack_kernel,
        [VMEM] * (1 + len(parts)),
        [VMEM] * 2,
        [shape((rows * len(parts), width)), shape(cot.shape)],
        "stack_rows",
    )(*parts, cot)


def tokens_kernel(row, row_place, col_place, *refs):
    *stacks, out, held = refs
    col, n = len(stacks), held.shape[1]
    my_row, my_col = row_place[0], col_place[0]
    for k, part in enumerate(stacks):
        rows = part[...].astype(jnp.float32)
        for r in range(row):
            at = lax.rem(my_row + row - r, row) * col + lax.rem(my_col + col - k, col)
            held[at] = rows[r * n : (r + 1) * n]
    for at in range(0, row * col, 2):
        pair = jnp.concatenate([held[at], held[at + 1]])
        out[at * n : (at + 2) * n] = pair.astype(out.dtype)


def tokens_in_order(row_place, col_place, stacks, row, after):
    rows, width = stacks[0].shape
    col = len(stacks)
    return call(
        functools.partial(tokens_kernel, row),
        [SMEM, SMEM] + [VMEM] * col,
        VMEM,
        shape((rows * col, width)),
        "order_tokens",
        scratch=[pltpu.VMEM((row * col, rows // row, width), jnp.float32)],
        after=after,
    )(row_place, col_place, *stacks)


def order_kernel(count, place, *refs):
    parts, outs, held = refs[:count], refs[count:-1], refs[-1]
    me, rows = place[0], parts[0].shape[0]
    for k, part in enumerate(parts):
        held[lax.rem(me + count - k, count)] = part[...]
    each = count // len(outs)
    for k in range(count):
        start = k % each * rows
        outs[k // each][start : start + rows] = held[k]


def in_order(col_place, parts, after):
    rows, width = parts[0].shape
    count = len(parts)
    return call(
        functools.partial(order_kernel, count),
        [SMEM] + [VMEM] * count,
        [VMEM] * COT_PIECES,
        [shape((rows * count // COT_PIECES, width))] * COT_PIECES,
        "order_rows",
        scratch=[pltpu.VMEM((count, rows, width), jnp.bfloat16)],
        after=after,
    )(col_place, *parts)


def first_kernel(dims, tile, mine, *refs):
    *groups, w, total, sent, own_out, rows = refs
    at = 0
    for i, group in enumerate(groups):
        cut = slice(at, at + group.shape[0])
        rows[cut] = group[...]
        if i < mine:
            own_out[cut] = group[...]
        at += group.shape[0]
    for at in range(0, total.shape[1], tile):
        cut = slice(at, at + tile)
        if dims is NN:
            part = mm(rows[...], w[:, cut], NN)
        else:
            part = mm_streamed(rows[...], w[cut, :])
        total[:, cut] = part
        sent[:, cut] = part.astype(jnp.bfloat16)


def first(own, other, w, dims, name):
    half, width = len(own) * own[0].shape[0], own[0].shape[1]
    n = 2 * half
    units = w.shape[1 if dims is NN else 0]
    tile = tile_of(units, 256 if dims is NN else 512)
    return call(
        functools.partial(first_kernel, dims, tile, len(own)),
        [VMEM] * (len(own) + len(other) + 1),
        [VMEM] * 3,
        [shape((n, units), jnp.float32), shape((n, units)), shape((half, width))],
        name,
        scratch=[pltpu.VMEM((n, width), jnp.bfloat16)],
    )(*own, *other, w)


def gelu_parts(preact):
    cdf = 0.5 * (1.0 + lax.erf(preact * 0.7071067811865476))
    slopes = cdf + preact * jnp.exp(-0.5 * preact * preact) * 0.3989422804014327
    return (preact * cdf, slopes)


def second_product(dims, vals, w, keep, sends):
    half, width = keep.shape
    tile = tile_of(width, 512)
    for at in range(0, width, tile):
        cut = slice(at, at + tile)
        if dims is NN:
            part = mm(vals[...], w[:, cut], NN)
        else:
            part = mm_streamed(vals[...], w[cut, :])
        keep[:, cut] = part[:half]
        for i, send in enumerate(sends):
            rows = send.shape[0]
            send[:, cut] = part[half + i * rows : half + (i + 1) * rows].astype(jnp.bfloat16)


def row_sum(total, parts, cut):
    whole = total[:, cut]
    for part in parts:
        whole = whole + part[:, cut].astype(jnp.float32)
    return whole


def forward_kernel(blocks, shares, *refs):
    total, parts, w = refs[0], refs[1 : 1 + shares], refs[1 + shares]
    keep, *sends = refs[2 + shares : 3 + shares + OUT_PIECES]
    slopes, *hidden, vals = refs[3 + shares + OUT_PIECES :]
    size = total.shape[1] // blocks
    for b in range(blocks):
        cut = slice(b * size, (b + 1) * size)
        value, slope = gelu_parts(row_sum(total, parts, cut))
        value = value.astype(jnp.bfloat16)
        vals[:, cut] = value
        hidden[b][...] = value
        slopes[:, cut] = slope
    second_product(NN, vals, w, keep, sends)


def block_out_partial(total, parts, w, size, after):
    n, units = total.shape
    half, blocks, width = n // 2, units // size, w.shape[1]
    out_shape = (
        [shape((half, width), jnp.float32)]
        + [shape((half // OUT_PIECES, width))] * OUT_PIECES
        + [shape((n, units), jnp.float32)]
        + [shape((n, size))] * blocks
    )
    keep, *rest = call(
        functools.partial(forward_kernel, blocks, len(parts)),
        [VMEM] * (2 + len(parts)),
        [VMEM] * len(out_shape),
        out_shape,
        "block_out_partial",
        scratch=[pltpu.VMEM((n, units), jnp.bfloat16)],
        after=after,
    )(total, *parts, w)
    return keep, rest[:OUT_PIECES], rest[OUT_PIECES], rest[OUT_PIECES + 1 :]


def backward_kernel(blocks, shares, *refs):
    total, parts, slopes, w = refs[0], refs[1 : 1 + shares], refs[1 + shares], refs[2 + shares]
    hidden, refs = refs[3 + shares : 2 + shares + blocks], refs[2 + shares + blocks :]
    keep, send, *pre = refs[: 2 + blocks]
    *handed_on, vals = refs[2 + blocks :]
    for a, b in zip(hidden, handed_on):
        b[...] = a[...]
    size = total.shape[1] // blocks
    for b in range(blocks):
        cut = slice(b * size, (b + 1) * size)
        value = (row_sum(total, parts, cut) * slopes[:, cut]).astype(jnp.bfloat16)
        vals[:, cut] = value
        pre[b][...] = value
    second_product(NT, vals, w, keep, [send])


def grad_in_partial(total, parts, slopes, w, hidden, size, after):
    n, units = total.shape
    half, blocks, width = n // 2, units // size, w.shape[0]
    out_shape = [shape((half, width), jnp.float32), shape((half, width))]
    out_shape += [shape((n, size))] * (blocks + len(hidden))
    keep, send, *rest = call(
        functools.partial(backward_kernel, blocks, len(parts)),
        [VMEM] * (3 + len(parts) + len(hidden)),
        [VMEM] * len(out_shape),
        out_shape,
        "grad_in_partial",
        scratch=[pltpu.VMEM((n, units), jnp.bfloat16)],
        after=after,
    )(total, *parts, slopes, w, *hidden)
    return keep, send, rest[:blocks], rest[blocks:]


def cores_kernel(pieces, count, steps, place, keep, *refs):
    parts, outs, held = refs[:pieces], refs[pieces:-1], refs[-1]
    rows = keep.shape[0] // count
    at = 0
    for part in parts:
        cut = slice(at, at + part.shape[0])
        held[cut] = keep[cut] + part[...].astype(jnp.float32)
        at += part.shape[0]
    for k, out in zip(steps, outs):
        at = pl.ds(pl.multiple_of(lax.rem(place[0] + k, count) * rows, 16), rows)
        out[...] = held[at].astype(out.dtype)


def cores_sum(col_place, keep, parts, count, steps, name, after=()):
    rows, width = keep.shape[0] // count, keep.shape[1]
    return call(
        functools.partial(cores_kernel, len(parts), count, steps),
        [SMEM, VMEM] + [VMEM] * len(parts),
        [VMEM] * len(steps),
        [shape((rows, width), jnp.bfloat16 if k else jnp.float32) for k in steps],
        name,
        scratch=[pltpu.VMEM(keep.shape, jnp.float32)],
        after=after,
    )(col_place, keep, *parts)


def weight_kernel(lefts, tile, across, *refs):
    left, right, out = refs[:lefts], refs[lefts:-5], refs[-5]
    rows_left, rows_right, staged, sems = refs[-4:]
    for groups, rows in ((left, rows_left), (right, rows_right)):
        at = 0
        for group in groups:
            rows[at : at + group.shape[0]] = group[...]
            at += group.shape[0]
    copies = []
    for i, at in enumerate(range(0, out.shape[1 if across else 0], tile)):
        cut = slice(at, at + tile)
        if across:
            part, where = mm(rows_left[...], rows_right[:, cut], TN), (slice(None), cut)
        else:
            part, where = mm(rows_left[:, cut], rows_right[...], TN), (cut, slice(None))
        staged[where] = part.astype(jnp.bfloat16)
        copies.append(pltpu.make_async_copy(staged.at[where], out.at[where], sems.at[i]))
        copies[-1].start()
    for copy in copies:
        copy.wait()


def weight_grad(left, right, across, name, after=()):
    n = sum(group.shape[0] for group in left)
    k, m = left[0].shape[1], right[0].shape[1]
    long = m if across else k
    tile = tile_of(long, 512)
    return call(
        functools.partial(weight_kernel, len(left), tile, across),
        [VMEM] * (len(left) + len(right)),
        HBM,
        shape((k, m)),
        name,
        scratch=[
            pltpu.VMEM((n, k), jnp.bfloat16),
            pltpu.VMEM((n, m), jnp.bfloat16),
            pltpu.VMEM((k, m), jnp.bfloat16),
            pltpu.SemaphoreType.DMA((long // tile,)),
        ],
        after=after,
    )(*left, *right)


def body(dp, row, col, tokens, w_in, w_out, grad_out):
    blocks = dp // CORES
    width, size = w_in.shape[0], w_in.shape[2] // dp
    dp_place = lax.axis_index("dp").astype(jnp.int32)[None]
    row_place = lax.axis_index("row").astype(jnp.int32)[None]
    col_place = lax.axis_index("col").astype(jnp.int32)[None]

    def shifted(x, axis, step):
        count = {"dp": dp, "row": row, "col": col}[axis]
        return lax.ppermute(x, axis, [(i, (i + step) % count) for i in range(count)])

    def across_cores(x):
        return lax.ppermute(x, "dp", [(i, i ^ 1) for i in range(dp)])

    def across_rows(x):
        return [shifted(x, "row", step) for step in range(1, row)]

    def across_chips(x):
        return [shifted(x, "dp", CORES * b) for b in range(1, blocks)]

    cot_mine, own, *other_widths = split(row_place, in_hbm(tokens), in_hbm(grad_out), row)
    arrived = [shifted(part, "row", step + 1) for step, part in enumerate(other_widths)]
    stacked, cot_mine = stack([own, *arrived], cot_mine)
    stacks = [stacked] + [shifted(stacked, "col", step) for step in range(1, col)]
    cots = [cot_mine] + [shifted(cot_mine, "col", step) for step in range(1, col)]
    w_first = load(dp_place, w_in[:, 0, :], dp, size, True, "load_first", [stacked])
    tok = tokens_in_order(row_place, col_place, stacks, row, [w_first])
    tok_other = across_cores(tok)

    pre_total, pre_sent, tok_later = first([tok], [tok_other], w_first, NN, "preact_partial")
    pre_parts = across_rows(pre_sent)
    w_second = load(dp_place, w_out[0], dp, size, False, "load_second", [pre_sent])
    cot = in_order(col_place, cots, [w_second])
    cot_other = [across_cores(x) for x in cot]
    back_total, back_sent, cot_later = first(cot, cot_other, w_second, NT, "back_partial")
    back_parts = across_rows(back_sent)
    tok_there = across_chips(tok_later)
    cot_there = across_chips(cot_later)

    far_first = sorted(range(1, col), key=lambda k: -min(k, col - k))

    def col_total(sums):
        total = sums[0]
        for part in [shifted(sums[k], "col", k) for k in far_first]:
            total = total + part.astype(jnp.float32)
        return total.astype(jnp.bfloat16)

    out_keep, out_sends, slopes, hidden = block_out_partial(
        pre_total, pre_parts, w_second, size, [back_sent]
    )
    out_parts = [across_cores(x) for x in out_sends]
    out_sums = cores_sum(col_place, out_keep, out_parts, col, range(col), "block_out_cores")
    block_out = col_total(out_sums)

    def all_replicas(own, other, there):
        groups = [own, *other]
        for part in there:
            groups += [part, across_cores(part)]
        return groups

    tok_all = all_replicas(tok_later, [tok_other], tok_there)
    cot_all = all_replicas(cot_later, cot_other, cot_there)
    in_keep, in_send, grad_pre, handed_on = grad_in_partial(
        back_total, back_parts, slopes, w_first, hidden[1:], size, [out_sums[0], tok_there[-1]]
    )

    def to_owner(others):
        return [shifted(x, "dp", CORES * (b + 1)) for b, x in enumerate(others)]

    hid_arrived = to_owner(handed_on)
    in_parts = [across_cores(in_send)]
    ahead = [1]
    late = [k for k in range(col) if k not in ahead]
    after = [block_out, cot_all[-1], tok_all[-1]]
    in_sums = dict(
        zip(ahead, cores_sum(col_place, in_keep, in_parts, col, ahead, "grad_in_ahead"))
    )
    in_sums.update(
        zip(late, cores_sum(col_place, in_keep, in_parts, col, late, "grad_in_cores", after))
    )
    grad_in = col_total(in_sums)

    pre_arrived = to_owner(grad_pre[1:])
    grad_out_w = weight_grad([hidden[0], *hid_arrived], cot_all, True, "grad_w_out")
    grad_in_w = weight_grad(tok_all, [grad_pre[0], *pre_arrived], False, "grad_w_in", [in_sums[0]])
    return block_out, grad_in, grad_in_w[:, None, :], grad_out_w[None]


def solution(mesh):
    in_specs = (
        P(("dp", "row", "col"), None),
        P("row", "col", None),
        P("col", None, "row"),
        P(("dp", "col"), "row"),
    )
    out_specs = (
        P(("dp", "col"), "row"),
        P(("dp", "col"), "row"),
        P("row", "col", "dp"),
        P("col", "dp", "row"),
    )
    sizes = (mesh.shape["dp"], mesh.shape["row"], mesh.shape["col"])
    return jax.shard_map(
        functools.partial(body, *sizes),
        mesh=mesh,
        in_specs=in_specs,
        out_specs=out_specs,
        check_vma=False,
    )
```

```python
import functools

import jax
import jax.numpy as jnp
from jax import lax
from jax.experimental import pallas as pl
from jax.experimental.pallas import tpu as pltpu
from jax.sharding import PartitionSpec as P

CORES = 2
OUT_PIECES = 2
COT_PIECES = 2
VMEM_LIMIT = 24 * 1024 * 1024
NT = (((1,), (1,)), ((), ()))
NN = (((1,), (0,)), ((), ()))
TN = (((0,), (0,)), ((), ()))
VMEM = pl.BlockSpec(memory_space=pltpu.VMEM)
SMEM = pl.BlockSpec(memory_space=pltpu.SMEM)
HBM = pl.BlockSpec(memory_space=pltpu.HBM)
ANY = pl.BlockSpec(memory_space=pl.ANY)


def mm(a, b, dims):
    return lax.dot_general(a, b, dims, preferred_element_type=jnp.float32)


def mm_streamed(rows, weights):
    return mm(weights, rows, NT).T


def tile_of(size, most):
    for tile in range(most, 0, -128):
        if size % tile == 0:
            return tile
    return size


def in_hbm(x):
    return pltpu.with_memory_space_constraint(x, pltpu.HBM)


def call(kernel, in_specs, out_specs, out_shape, name, scratch=(), after=()):
    reads = len(in_specs)

    def run(*refs):
        kernel(*refs[:reads], *refs[reads + len(after) :])

    kernel_call = pl.pallas_call(
        run,
        in_specs=list(in_specs) + [ANY] * len(after),
        out_specs=out_specs,
        out_shape=out_shape,
        scratch_shapes=scratch,
        compiler_params=pltpu.CompilerParams(vmem_limit_bytes=VMEM_LIMIT),
        cost_estimate=pl.CostEstimate(flops=0, bytes_accessed=0, transcendentals=0),
        name=name,
    )
    return lambda *args: kernel_call(*args, *after)


def shape(dims, dtype=jnp.bfloat16):
    return jax.ShapeDtypeStruct(tuple(dims), dtype)


def load_kernel(dp, size, pieces, columns, place, w, out, sems):
    rows = (w.shape[0] if columns else size) // pieces
    copies = []
    for b in range(dp // CORES):
        start = lax.rem(place[0] + CORES * b, dp) * size
        for p in range(pieces):
            if columns:
                cut = pl.ds(p * rows, rows)
                source = w.at[cut, pl.ds(pl.multiple_of(start, 128), size)]
                to = out.at[cut, pl.ds(b * size, size)]
            else:
                source = w.at[pl.ds(pl.multiple_of(start + p * rows, 16), rows)]
                to = out.at[pl.ds(b * size + p * rows, rows)]
            copies.append(pltpu.make_async_copy(source, to, sems.at[b * pieces + p]))
    for copy in copies:
        copy.start()
    for copy in copies:
        copy.wait()


def load(place, w, dp, size, columns, name, after):
    blocks, pieces = dp // CORES, 4
    units = blocks * size
    return call(
        functools.partial(load_kernel, dp, size, pieces, columns),
        [SMEM, HBM],
        VMEM,
        pltpu.VMEM((w.shape[0], units) if columns else (units, w.shape[1]), jnp.bfloat16),
        name,
        scratch=[pltpu.SemaphoreType.DMA((blocks * pieces,))],
        after=after,
    )(place, in_hbm(w))


def split_kernel(place, tokens, cots, cot, *rest):
    *outs, sems = rest
    count, width = len(outs), outs[0].shape[1]
    copies = [pltpu.make_async_copy(cots, cot, sems.at[count])]
    for k in reversed(range(count)):
        at = lax.rem(place[0] + k, count) * width
        source = tokens.at[:, pl.ds(pl.multiple_of(at, 128), width)]
        copies.append(pltpu.make_async_copy(source, outs[k], sems.at[k]))
    for copy in reversed(copies):
        copy.start()
    for copy in copies:
        copy.wait()


def split(row_place, tokens, cots, count):
    rows, width = tokens.shape[0], tokens.shape[1] // count
    return call(
        split_kernel,
        [SMEM, HBM, HBM],
        [VMEM] * (1 + count),
        [shape(cots.shape)] + [shape((rows, width))] * count,
        "split_width",
        scratch=[pltpu.SemaphoreType.DMA((1 + count,))],
    )(row_place, tokens, cots)


def stack_kernel(*refs):
    *parts, cot, out, cot_out = refs
    out[...] = jnp.concatenate([r[...].astype(jnp.float32) for r in parts]).astype(out.dtype)
    cot_out[...] = cot[...]


def stack(parts, cot):
    rows, width = parts[0].shape
    return call(
        stack_kernel,
        [VMEM] * (1 + len(parts)),
        [VMEM] * 2,
        [shape((rows * len(parts), width)), shape(cot.shape)],
        "stack_rows",
    )(*parts, cot)


def tokens_kernel(row, row_place, col_place, *refs):
    *stacks, out, held = refs
    col, n = len(stacks), held.shape[1]
    my_row, my_col = row_place[0], col_place[0]
    for k, part in enumerate(stacks):
        rows = part[...].astype(jnp.float32)
        for r in range(row):
            at = lax.rem(my_row + row - r, row) * col + lax.rem(my_col + col - k, col)
            held[at] = rows[r * n : (r + 1) * n]
    for at in range(0, row * col, 2):
        pair = jnp.concatenate([held[at], held[at + 1]])
        out[at * n : (at + 2) * n] = pair.astype(out.dtype)


def tokens_in_order(row_place, col_place, stacks, row, after):
    rows, width = stacks[0].shape
    col = len(stacks)
    return call(
        functools.partial(tokens_kernel, row),
        [SMEM, SMEM] + [VMEM] * col,
        VMEM,
        shape((rows * col, width)),
        "order_tokens",
        scratch=[pltpu.VMEM((row * col, rows // row, width), jnp.float32)],
        after=after,
    )(row_place, col_place, *stacks)


def order_kernel(count, place, *refs):
    parts, outs, held = refs[:count], refs[count:-1], refs[-1]
    me, rows = place[0], parts[0].shape[0]
    for k, part in enumerate(parts):
        held[lax.rem(me + count - k, count)] = part[...]
    each = count // len(outs)
    for k in range(count):
        start = k % each * rows
        outs[k // each][start : start + rows] = held[k]


def in_order(col_place, parts, after):
    rows, width = parts[0].shape
    count = len(parts)
    return call(
        functools.partial(order_kernel, count),
        [SMEM] + [VMEM] * count,
        [VMEM] * COT_PIECES,
        [shape((rows * count // COT_PIECES, width))] * COT_PIECES,
        "order_rows",
        scratch=[pltpu.VMEM((count, rows, width), jnp.bfloat16)],
        after=after,
    )(col_place, *parts)


def first_kernel(dims, tile, mine, *refs):
    *groups, w, total, sent, own_out, rows = refs
    at = 0
    for i, group in enumerate(groups):
        cut = slice(at, at + group.shape[0])
        rows[cut] = group[...]
        if i < mine:
            own_out[cut] = group[...]
        at += group.shape[0]
    for at in range(0, total.shape[1], tile):
        cut = slice(at, at + tile)
        if dims is NN:
            part = mm(rows[...], w[:, cut], NN)
        else:
            part = mm_streamed(rows[...], w[cut, :])
        total[:, cut] = part
        sent[:, cut] = part.astype(jnp.bfloat16)


def first(own, other, w, dims, name):
    half, width = len(own) * own[0].shape[0], own[0].shape[1]
    n = 2 * half
    units = w.shape[1 if dims is NN else 0]
    tile = tile_of(units, 256 if dims is NN else 512)
    return call(
        functools.partial(first_kernel, dims, tile, len(own)),
        [VMEM] * (len(own) + len(other) + 1),
        [VMEM] * 3,
        [shape((n, units), jnp.float32), shape((n, units)), shape((half, width))],
        name,
        scratch=[pltpu.VMEM((n, width), jnp.bfloat16)],
    )(*own, *other, w)


def gelu_parts(preact):
    cdf = 0.5 * (1.0 + lax.erf(preact * 0.7071067811865476))
    slopes = cdf + preact * jnp.exp(-0.5 * preact * preact) * 0.3989422804014327
    return (preact * cdf, slopes)


def second_product(dims, vals, w, keep, sends):
    half, width = keep.shape
    tile = tile_of(width, 1024)
    for at in range(0, width, tile):
        cut = slice(at, at + tile)
        if dims is NN:
            part = mm(vals[...], w[:, cut], NN)
        else:
            part = mm_streamed(vals[...], w[cut, :])
        keep[:, cut] = part[:half]
        for i, send in enumerate(sends):
            rows = send.shape[0]
            send[:, cut] = part[half + i * rows : half + (i + 1) * rows].astype(jnp.bfloat16)


def row_sum(total, parts, cut):
    whole = total[:, cut]
    for part in parts:
        whole = whole + part[:, cut].astype(jnp.float32)
    return whole


def forward_kernel(blocks, shares, *refs):
    total, parts, w = refs[0], refs[1 : 1 + shares], refs[1 + shares]
    keep, *sends = refs[2 + shares : 3 + shares + OUT_PIECES]
    slopes, *hidden, vals = refs[3 + shares + OUT_PIECES :]
    size = total.shape[1] // blocks
    for b in range(blocks):
        cut = slice(b * size, (b + 1) * size)
        value, slope = gelu_parts(row_sum(total, parts, cut))
        value = value.astype(jnp.bfloat16)
        vals[:, cut] = value
        hidden[b][...] = value
        slopes[:, cut] = slope
    second_product(NN, vals, w, keep, sends)


def block_out_partial(total, parts, w, size, after):
    n, units = total.shape
    half, blocks, width = n // 2, units // size, w.shape[1]
    out_shape = (
        [shape((half, width), jnp.float32)]
        + [shape((half // OUT_PIECES, width))] * OUT_PIECES
        + [shape((n, units), jnp.float32)]
        + [shape((n, size))] * blocks
    )
    keep, *rest = call(
        functools.partial(forward_kernel, blocks, len(parts)),
        [VMEM] * (2 + len(parts)),
        [VMEM] * len(out_shape),
        out_shape,
        "block_out_partial",
        scratch=[pltpu.VMEM((n, units), jnp.bfloat16)],
        after=after,
    )(total, *parts, w)
    return keep, rest[:OUT_PIECES], rest[OUT_PIECES], rest[OUT_PIECES + 1 :]


def backward_kernel(blocks, shares, *refs):
    total, parts, slopes, w = refs[0], refs[1 : 1 + shares], refs[1 + shares], refs[2 + shares]
    hidden, refs = refs[3 + shares : 2 + shares + blocks], refs[2 + shares + blocks :]
    keep, send, *pre = refs[: 2 + blocks]
    *handed_on, vals = refs[2 + blocks :]
    for a, b in zip(hidden, handed_on):
        b[...] = a[...]
    size = total.shape[1] // blocks
    for b in range(blocks):
        cut = slice(b * size, (b + 1) * size)
        value = (row_sum(total, parts, cut) * slopes[:, cut]).astype(jnp.bfloat16)
        vals[:, cut] = value
        pre[b][...] = value
    second_product(NT, vals, w, keep, [send])


def grad_in_partial(total, parts, slopes, w, hidden, size, after):
    n, units = total.shape
    half, blocks, width = n // 2, units // size, w.shape[0]
    out_shape = [shape((half, width), jnp.float32), shape((half, width))]
    out_shape += [shape((n, size))] * (blocks + len(hidden))
    keep, send, *rest = call(
        functools.partial(backward_kernel, blocks, len(parts)),
        [VMEM] * (3 + len(parts) + len(hidden)),
        [VMEM] * len(out_shape),
        out_shape,
        "grad_in_partial",
        scratch=[pltpu.VMEM((n, units), jnp.bfloat16)],
        after=after,
    )(total, *parts, slopes, w, *hidden)
    return keep, send, rest[:blocks], rest[blocks:]


def cores_kernel(pieces, count, steps, place, keep, *refs):
    parts, outs, held = refs[:pieces], refs[pieces:-1], refs[-1]
    rows = keep.shape[0] // count
    at = 0
    for part in parts:
        cut = slice(at, at + part.shape[0])
        held[cut] = keep[cut] + part[...].astype(jnp.float32)
        at += part.shape[0]
    for k, out in zip(steps, outs):
        at = pl.ds(pl.multiple_of(lax.rem(place[0] + k, count) * rows, 16), rows)
        out[...] = held[at].astype(out.dtype)


def cores_sum(col_place, keep, parts, count, steps, name, after=()):
    rows, width = keep.shape[0] // count, keep.shape[1]
    return call(
        functools.partial(cores_kernel, len(parts), count, steps),
        [SMEM, VMEM] + [VMEM] * len(parts),
        [VMEM] * len(steps),
        [shape((rows, width), jnp.bfloat16 if k else jnp.float32) for k in steps],
        name,
        scratch=[pltpu.VMEM(keep.shape, jnp.float32)],
        after=after,
    )(col_place, keep, *parts)


def weight_kernel(lefts, tile, across, *refs):
    left, right, out = refs[:lefts], refs[lefts:-5], refs[-5]
    rows_left, rows_right, staged, sems = refs[-4:]
    for groups, rows in ((left, rows_left), (right, rows_right)):
        at = 0
        for group in groups:
            rows[at : at + group.shape[0]] = group[...]
            at += group.shape[0]
    copies = []
    for i, at in enumerate(range(0, out.shape[1 if across else 0], tile)):
        cut = slice(at, at + tile)
        if across:
            part, where = mm(rows_left[...], rows_right[:, cut], TN), (slice(None), cut)
        else:
            part, where = mm(rows_left[:, cut], rows_right[...], TN), (cut, slice(None))
        staged[where] = part.astype(jnp.bfloat16)
        copies.append(pltpu.make_async_copy(staged.at[where], out.at[where], sems.at[i]))
        copies[-1].start()
    for copy in copies:
        copy.wait()


def weight_grad(left, right, across, name, after=()):
    n = sum(group.shape[0] for group in left)
    k, m = left[0].shape[1], right[0].shape[1]
    long = m if across else k
    tile = tile_of(long, 512)
    return call(
        functools.partial(weight_kernel, len(left), tile, across),
        [VMEM] * (len(left) + len(right)),
        HBM,
        shape((k, m)),
        name,
        scratch=[
            pltpu.VMEM((n, k), jnp.bfloat16),
            pltpu.VMEM((n, m), jnp.bfloat16),
            pltpu.VMEM((k, m), jnp.bfloat16),
            pltpu.SemaphoreType.DMA((long // tile,)),
        ],
        after=after,
    )(*left, *right)


def body(dp, row, col, tokens, w_in, w_out, grad_out):
    blocks = dp // CORES
    width, size = w_in.shape[0], w_in.shape[2] // dp
    dp_place = lax.axis_index("dp").astype(jnp.int32)[None]
    row_place = lax.axis_index("row").astype(jnp.int32)[None]
    col_place = lax.axis_index("col").astype(jnp.int32)[None]

    def shifted(x, axis, step):
        count = {"dp": dp, "row": row, "col": col}[axis]
        return lax.ppermute(x, axis, [(i, (i + step) % count) for i in range(count)])

    def across_cores(x):
        return lax.ppermute(x, "dp", [(i, i ^ 1) for i in range(dp)])

    def across_rows(x):
        return [shifted(x, "row", step) for step in range(1, row)]

    def across_chips(x):
        return [shifted(x, "dp", CORES * b) for b in range(1, blocks)]

    cot_mine, own, *other_widths = split(row_place, in_hbm(tokens), in_hbm(grad_out), row)
    arrived = [shifted(part, "row", step + 1) for step, part in enumerate(other_widths)]
    stacked, cot_mine = stack([own, *arrived], cot_mine)
    stacks = [stacked] + [shifted(stacked, "col", step) for step in range(1, col)]
    cots = [cot_mine] + [shifted(cot_mine, "col", step) for step in range(1, col)]
    w_first = load(dp_place, w_in[:, 0, :], dp, size, True, "load_first", [stacked])
    tok = tokens_in_order(row_place, col_place, stacks, row, [w_first])
    tok_other = across_cores(tok)

    pre_total, pre_sent, tok_later = first([tok], [tok_other], w_first, NN, "preact_partial")
    pre_parts = across_rows(pre_sent)
    w_second = load(dp_place, w_out[0], dp, size, False, "load_second", [pre_sent])
    cot = in_order(col_place, cots, [w_second])
    cot_other = [across_cores(x) for x in cot]
    back_total, back_sent, cot_later = first(cot, cot_other, w_second, NT, "back_partial")
    back_parts = across_rows(back_sent)
    tok_there = across_chips(tok_later)
    cot_there = across_chips(cot_later)

    far_first = sorted(range(1, col), key=lambda k: -min(k, col - k))

    def col_total(sums):
        total = sums[0]
        for part in [shifted(sums[k], "col", k) for k in far_first]:
            total = total + part.astype(jnp.float32)
        return total.astype(jnp.bfloat16)

    out_keep, out_sends, slopes, hidden = block_out_partial(
        pre_total, pre_parts, w_second, size, [back_sent]
    )
    out_parts = [across_cores(x) for x in out_sends]
    out_sums = cores_sum(col_place, out_keep, out_parts, col, range(col), "block_out_cores")
    block_out = col_total(out_sums)

    def all_replicas(own, other, there):
        groups = [own, *other]
        for part in there:
            groups += [part, across_cores(part)]
        return groups

    tok_all = all_replicas(tok_later, [tok_other], tok_there)
    cot_all = all_replicas(cot_later, cot_other, cot_there)
    in_keep, in_send, grad_pre, handed_on = grad_in_partial(
        back_total, back_parts, slopes, w_first, hidden[1:], size, [out_sums[0], tok_there[-1]]
    )

    def to_owner(others):
        return [shifted(x, "dp", CORES * (b + 1)) for b, x in enumerate(others)]

    hid_arrived = to_owner(handed_on)
    in_parts = [across_cores(in_send)]
    ahead = [1]
    late = [k for k in range(col) if k not in ahead]
    after = [block_out, cot_all[-1], tok_all[-1]]
    in_sums = dict(
        zip(ahead, cores_sum(col_place, in_keep, in_parts, col, ahead, "grad_in_ahead"))
    )
    in_sums.update(
        zip(late, cores_sum(col_place, in_keep, in_parts, col, late, "grad_in_cores", after))
    )
    grad_in = col_total(in_sums)

    pre_arrived = to_owner(grad_pre[1:])
    grad_out_w = weight_grad([hidden[0], *hid_arrived], cot_all, True, "grad_w_out")
    grad_in_w = weight_grad(tok_all, [grad_pre[0], *pre_arrived], False, "grad_w_in", [in_sums[0]])
    return block_out, grad_in, grad_in_w[:, None, :], grad_out_w[None]


def solution(mesh):
    in_specs = (
        P(("dp", "row", "col"), None),
        P("row", "col", None),
        P("col", None, "row"),
        P(("dp", "col"), "row"),
    )
    out_specs = (
        P(("dp", "col"), "row"),
        P(("dp", "col"), "row"),
        P("row", "col", "dp"),
        P("col", "dp", "row"),
    )
    sizes = (mesh.shape["dp"], mesh.shape["row"], mesh.shape["col"])
    return jax.shard_map(
        functools.partial(body, *sizes),
        mesh=mesh,
        in_specs=in_specs,
        out_specs=out_specs,
        check_vma=False,
    )
```
